512 devices in a mesh: band: 2 (over x_lo), dx: 16 (over z), dy: 16 (over y, x_hi, core).
Axes of the slice: x: 4 (x_hi: 2, x_lo: 2; x = x_hi * 2 + x_lo), y: 4, z: 16, core: 2. Of those that a mesh axis runs over, the one named last changes fastest.
Arguments:
- orbital_block: float32 [16, 192, 128, 128], P('band', 'dx', 'dy'), may hold values from -6 to 6
- potential: float32 [192, 128, 128], P('dx', 'dy'), may hold values from -2 to 0
- resident: bfloat16 [256, 192, 128, 128], P('band', 'dx', 'dy'), may hold values from -0.01953125 to 0.01953125
Outputs:
- projected_block: float32 [16, 192, 128, 128], P('band', 'dx', 'dy')
- block_gram: float32 [16, 16], P('band')
The draws below stay inside these ranges and needn't reach their ends.
All inputs are finite; a program needn't handle non-finite values.
Results may differ from the reference program's by a relative error of at most 0.0035.
Values may be sent and summed in bfloat16 or wider, within the bound.
No kernel may reach another device: no remote copies, remote signals or barrier semaphores. Data moves between devices by JAX's collectives and lax.ppermute only.
A program may use at most 64 MiB of HBM per device.

```python
import jax
import jax.numpy as jnp
from jax import lax

NB = 16
NRES = 256
DEGREE = 4
NZ = 128
NX = 192
NY = 128


def level_of(own_key, dims, shards, smallest, top_value):
    gain, own = 1.0, jax.random.fold_in(own_key, 6)
    for axis_at, shards_of in shards:
        steps = jnp.exp(jax.random.uniform(jax.random.fold_in(own, axis_at), (shards_of,), jnp.float32, smallest / len(shards), top_value / len(shards)))
        gain = gain * jnp.repeat(steps, dims[axis_at] // shards_of).reshape([-1 if axis == axis_at else 1 for axis in range(len(dims))])
    return gain


def normal_values(key, extent, deviation, reach, pieces=(), dtype=jnp.bfloat16):
    array = deviation * jax.random.normal(key, extent, jnp.float32)
    if pieces:
        array = array * level_of(key, extent, pieces, -0.22, 0.18)
    return jnp.clip(array, -reach, reach).astype(dtype)


def setup_inputs(seed: int = 0) -> dict:
    keys = jax.random.split(jax.random.key(seed), 4)
    orbital_block = normal_values(keys[0], (NB, NX, NY, NZ), 1.0, 6.0, ((0, 2), (1, 16), (2, 16)), jnp.float32)
    potential = jnp.clip(-2.0 + 2.0 * jax.random.uniform(keys[1], (NX, NY, NZ), jnp.float32) ** level_of(keys[1], (NX, NY, NZ), ((0, 16), (1, 16)), -0.2, 0.2), -2.0, 0.0)
    resident = normal_values(keys[2], (NRES, NX, NY, NZ), (0.14 * (NX * NY * NZ) ** -0.25), 0.01953125, ((0, 2), (1, 16), (2, 16)))
    return {"orbital_block": orbital_block, "potential": potential, "resident": resident}


STENCIL_WEIGHTS = (-5369.0 / 1800.0, 12.0 / 7.0, -15.0 / 56.0, 10.0 / 189.0, -1.0 / 112.0, 2.0 / 1925.0, -1.0 / 16632.0)
FILTER_CENTER = 23.0
FILTER_HALF = 21.0


def apply_hamiltonian(orbital_field, potential):
    depth_cells = orbital_field.shape[2]
    zpadded = jnp.pad(orbital_field, ((0, 0), (0, 0), (6, 6)))
    stencil_sum = 3.0 * STENCIL_WEIGHTS[0] * orbital_field
    for offset in range(1, 7):
        beside_all = jnp.roll(orbital_field, offset, 0) + jnp.roll(orbital_field, -offset, 0)
        beside_all = beside_all + jnp.roll(orbital_field, offset, 1) + jnp.roll(orbital_field, -offset, 1)
        beside_all = beside_all + zpadded[:, :, 6 + offset:6 + offset + depth_cells] + zpadded[:, :, 6 - offset:6 - offset + depth_cells]
        stencil_sum = stencil_sum + STENCIL_WEIGHTS[offset] * beside_all
    return -2.0 * stencil_sum + potential * orbital_field


def shifted(orbital_field, potential):
    return (apply_hamiltonian(orbital_field, potential) - FILTER_CENTER * orbital_field) / FILTER_HALF


def reference(orbital_block, potential, resident):
    def filter_one(orbital):
        previous = orbital
        current = shifted(orbital, potential)
        for degree_step in range(DEGREE - 1):
            following = 2.0 * shifted(current, potential) - previous
            previous, current = current, following
        return current

    filtered = lax.map(filter_one, orbital_block)
    total_cells = NX * NY * NZ
    flattened = filtered.reshape(NB, total_cells)
    rounded = flattened.astype(jnp.bfloat16)
    orbitals = resident.reshape(NRES, total_cells)
    correlations = jnp.dot(orbitals, rounded.T, preferred_element_type=jnp.float32)
    correction = jnp.dot(correlations.astype(jnp.bfloat16).T, orbitals, preferred_element_type=jnp.float32)
    projected = flattened - correction
    gram_matrix = jnp.dot(projected, projected.T, precision=lax.Precision.HIGHEST, preferred_element_type=jnp.float32) / total_cells
    return projected.reshape(NB, NX, NY, NZ), gram_matrix
```

```python
import jax
import jax.numpy as jnp
from jax import lax
from jax.sharding import PartitionSpec as P

DEGREE = 4


STENCIL_WEIGHTS = (
    -5369.0 / 1800.0,
    12.0 / 7.0,
    -15.0 / 56.0,
    10.0 / 189.0,
    -1.0 / 112.0,
    2.0 / 1925.0,
    -1.0 / 16632.0,
)
FILTER_CENTER = 23.0
FILTER_HALF = 21.0
WIDTH = 6


def neighbour_layers(cells, axis, dim):
    count = lax.axis_size(axis)
    size = cells.shape[dim]
    high = cells.astype(jnp.bfloat16)

    def packed(start, near):
        layers = lax.slice_in_dim(high, start, start + WIDTH, axis=dim)
        edge = lax.slice_in_dim(cells, near, near + 1, axis=dim)
        rest = edge - lax.slice_in_dim(high, near, near + 1, axis=dim).astype(jnp.float32)
        return jnp.concatenate([layers, rest.astype(jnp.bfloat16)], axis=dim)

    tail = lax.ppermute(
        packed(size - WIDTH, size - 1), axis, [(i, (i + 1) % count) for i in range(count)]
    )
    head = lax.ppermute(packed(0, 0), axis, [((i + 1) % count, i) for i in range(count)])

    def unpacked(got, near):
        layers = lax.slice_in_dim(got, 0, WIDTH, axis=dim).astype(jnp.float32)
        rest = lax.slice_in_dim(got, WIDTH, WIDTH + 1, axis=dim).astype(jnp.float32)
        pads = [(0, 0)] * got.ndim
        pads[dim] = (near, WIDTH - 1 - near)
        return layers + jnp.pad(rest, pads)

    return unpacked(tail, WIDTH - 1), unpacked(head, 0)


def apply_hamiltonian(orbital_field, potential):
    rows_x, rows_y, depth_cells = orbital_field.shape[1:]
    left, right = neighbour_layers(orbital_field, "dx", 1)
    below, above = neighbour_layers(orbital_field, "dy", 2)
    along_x = jnp.concatenate([left, orbital_field, right], axis=1)
    along_y = jnp.concatenate([below, orbital_field, above], axis=2)
    along_z = jnp.pad(orbital_field, ((0, 0), (0, 0), (0, 0), (WIDTH, WIDTH)))
    stencil_sum = 3.0 * STENCIL_WEIGHTS[0] * orbital_field
    for offset in range(1, WIDTH + 1):
        lo, hi = WIDTH - offset, WIDTH + offset
        beside_all = (
            along_x[:, lo : lo + rows_x]
            + along_x[:, hi : hi + rows_x]
            + along_y[:, :, lo : lo + rows_y]
            + along_y[:, :, hi : hi + rows_y]
            + along_z[:, :, :, lo : lo + depth_cells]
            + along_z[:, :, :, hi : hi + depth_cells]
        )
        stencil_sum = stencil_sum + STENCIL_WEIGHTS[offset] * beside_all
    return -2.0 * stencil_sum + potential[None] * orbital_field


def shifted(orbital_field, potential):
    return (
        apply_hamiltonian(orbital_field, potential) - FILTER_CENTER * orbital_field
    ) / FILTER_HALF


def sum_over_grid(values):
    for axis in ("dx", "dy"):
        count = lax.axis_size(axis)
        sent = jnp.broadcast_to(values[None], (count,) + values.shape)
        values = jnp.sum(lax.all_to_all(sent, axis, 0, 0), axis=0)
    return values


def other_band(values):
    return lax.ppermute(values, "band", [(0, 1), (1, 0)])


def shards(orbital_block, potential, resident):
    previous = orbital_block
    current = shifted(orbital_block, potential)
    for degree_step in range(DEGREE - 1):
        following = 2.0 * shifted(current, potential) - previous
        previous, current = (current, following)
    own_count = current.shape[0]
    cell_count = current.shape[1] * current.shape[2] * current.shape[3]
    filtered = current.reshape(own_count, cell_count)
    rounded = filtered.astype(jnp.bfloat16)
    rounded_other = other_band(rounded)
    own_resident = resident.reshape(-1, cell_count)
    both = jnp.concatenate([rounded, rounded_other], axis=0)
    local = lax.dot_general(
        both, own_resident, (((1,), (1,)), ((), ())), preferred_element_type=jnp.float32
    )
    correlations = sum_over_grid(local).astype(jnp.bfloat16)
    correction = jnp.dot(correlations, own_resident, preferred_element_type=jnp.float32)
    mine, theirs = correction[:own_count], correction[own_count:]
    sent = jnp.concatenate([theirs, mine], axis=0).astype(jnp.bfloat16)
    got = other_band(sent).astype(jnp.float32)
    projected = filtered - mine - got[:own_count]
    projected_other = rounded_other.astype(jnp.float32) - theirs - got[own_count:]
    partial_own = lax.dot_general(
        projected,
        projected,
        (((1,), (1,)), ((), ())),
        precision=lax.Precision.HIGHEST,
        preferred_element_type=jnp.float32,
    )
    partial_other = lax.dot_general(
        projected,
        projected_other,
        (((1,), (1,)), ((), ())),
        precision=lax.Precision.HIGHEST,
        preferred_element_type=jnp.float32,
    )
    first = jnp.concatenate([partial_own, partial_other], axis=1)
    second = jnp.concatenate([partial_other, partial_own], axis=1)
    partial_gram = jnp.where(lax.axis_index("band") == 0, first, second)
    total_cells = cell_count * lax.axis_size("dx") * lax.axis_size("dy")
    gram_matrix = sum_over_grid(partial_gram) / total_cells
    return (projected.reshape(current.shape), gram_matrix)


def solution(mesh):
    placed = (P("band", "dx", "dy", None), P("dx", "dy", None), P("band", "dx", "dy", None))
    return jax.shard_map(
        shards,
        mesh=mesh,
        in_specs=placed,
        out_specs=(P("band", "dx", "dy", None), P("band", None)),
        check_vma=False,
    )
```

```python
import functools

import jax
import jax.numpy as jnp
from jax import lax
from jax.experimental import pallas as pl
from jax.experimental.pallas import tpu as pltpu
from jax.sharding import PartitionSpec as P

DEGREE = 4


STENCIL_WEIGHTS = (
    -5369.0 / 1800.0,
    12.0 / 7.0,
    -15.0 / 56.0,
    10.0 / 189.0,
    -1.0 / 112.0,
    2.0 / 1925.0,
    -1.0 / 16632.0,
)
FILTER_CENTER = 23.0
FILTER_HALF = 21.0
WIDTH = 6
SENT = WIDTH + 1
VMEM_BYTES = 24 * 1024 * 1024


def pack_layer(out_ref, at, layer):
    rows = layer.shape[0] * layer.shape[1]
    out_ref[at * rows : (at + 1) * rows, :] = layer.reshape(rows, layer.shape[2]).astype(
        jnp.bfloat16
    )


def pack_halos(field_ref, to_left, to_right, to_below, to_above):
    size_x, size_y = field_ref.shape[:2]
    for at in range(WIDTH):
        pack_layer(to_left, at, field_ref[at])
        pack_layer(to_right, at, field_ref[size_x - WIDTH + at])
        pack_layer(to_below, at, field_ref[:, at])
        pack_layer(to_above, at, field_ref[:, size_y - WIDTH + at])
    for out_ref, layer in (
        (to_left, field_ref[0]),
        (to_right, field_ref[size_x - 1]),
        (to_below, field_ref[:, 0]),
        (to_above, field_ref[:, size_y - 1]),
    ):
        pack_layer(out_ref, WIDTH, layer - layer.astype(jnp.bfloat16).astype(jnp.float32))


def start_kernel(cells_ref, field_ref, *halo_refs):
    size_x, size_y, own = field_ref.shape[:3]
    for x in range(size_x):
        for y in range(size_y):
            rows = pl.ds(x * size_y + y, own, stride=size_x * size_y)
            field_ref[x, y] = cells_ref[rows, :]
    pack_halos(field_ref, *halo_refs)


def layer_of(halo_ref, at, near, shape):
    rows = shape[0] * shape[1]
    layer = halo_ref[at * rows : (at + 1) * rows, :].astype(jnp.float32)
    if at == near:
        layer = layer + halo_ref[WIDTH * rows : SENT * rows, :].astype(jnp.float32)
    return layer.reshape(shape)


def step_kernel(scale, has_previous, last, extras, *refs):
    field_ref, potential_ref, left, right, below, above = refs[:6]
    at = 6
    previous_ref = None
    if has_previous:
        previous_ref = refs[at]
        at += 1
    at += extras
    outs = refs[at:-2]
    along_x, along_y = refs[-2:]
    size_x, size_y, own, depth = field_ref.shape
    layer_x, layer_y = (size_y, own, depth), (size_x, own, depth)
    for k in range(WIDTH):
        along_x[k] = layer_of(left, k, WIDTH - 1, layer_x)
        along_x[WIDTH + size_x + k] = layer_of(right, k, 0, layer_x)
        along_y[:, k] = layer_of(below, k, WIDTH - 1, layer_y)
        along_y[:, WIDTH + size_y + k] = layer_of(above, k, 0, layer_y)
    along_x[WIDTH : WIDTH + size_x] = field_ref[...]
    along_y[:, WIDTH : WIDTH + size_y] = field_ref[...]

    weights = [-2.0 * scale * w for w in STENCIL_WEIGHTS]
    middle = 3.0 * weights[0] - scale * FILTER_CENTER
    lane = lax.broadcasted_iota(jnp.int32, (1, depth), 1)
    up = [None] + [jnp.where(lane >= k, weights[k], 0.0) for k in range(1, WIDTH + 1)]
    down = [None] + [jnp.where(lane < depth - k, weights[k], 0.0) for k in range(1, WIDTH + 1)]

    @pl.loop(0, size_x)
    def _(x):
        for y in range(size_y):
            centre = along_y[x, WIDTH + y]
            factor = middle + scale * potential_ref[pl.ds(x * size_y + y, 1), :]
            total = factor * centre
            if has_previous:
                total = total - previous_ref[x, y]
            for k in range(1, WIDTH + 1):
                beside = (along_x[x + WIDTH + k, y] + along_x[x + WIDTH - k, y]) + (
                    along_y[x, WIDTH + y + k] + along_y[x, WIDTH + y - k]
                )
                total = total + weights[k] * beside
                total = total + up[k] * pltpu.roll(centre, k, 1)
                total = total + down[k] * pltpu.roll(centre, depth - k, 1)
            if last:
                outs[0][pl.ds(x * size_y + y, own, stride=size_x * size_y), :] = total
            else:
                outs[0][x, y] = total

    if not last:
        pack_halos(*outs)


def halo_shapes(size_x, size_y, own, depth):
    to_x = jax.ShapeDtypeStruct((SENT * size_y * own, depth), jnp.bfloat16)
    to_y = jax.ShapeDtypeStruct((SENT * size_x * own, depth), jnp.bfloat16)
    return [to_x, to_x, to_y, to_y]


def params():
    return pltpu.CompilerParams(vmem_limit_bytes=VMEM_BYTES)


def start(orbital_block):
    own, size_x, size_y, depth = orbital_block.shape
    field = jax.ShapeDtypeStruct((size_x, size_y, own, depth), jnp.float32)
    return pl.pallas_call(
        start_kernel,
        out_shape=[field] + halo_shapes(size_x, size_y, own, depth),
        compiler_params=params(),
    )(orbital_block.reshape(own * size_x * size_y, depth))


def filter_step(field, potential, halos, previous, last, extras=()):
    size_x, size_y, own, depth = field.shape
    scale = (1.0 if previous is None else 2.0) / FILTER_HALF
    if last:
        out_shape = [jax.ShapeDtypeStruct((own * size_x * size_y, depth), jnp.float32)]
    else:
        out_shape = [jax.ShapeDtypeStruct(field.shape, jnp.float32)]
        out_shape += halo_shapes(size_x, size_y, own, depth)
    before = [] if previous is None else [previous]
    vmem = pl.BlockSpec(memory_space=pltpu.VMEM)
    return pl.pallas_call(
        functools.partial(step_kernel, scale, previous is not None, last, len(extras)),
        out_shape=out_shape,
        in_specs=[vmem] * (6 + len(before)) + [pl.BlockSpec(memory_space=pl.ANY)] * len(extras),
        out_specs=[vmem] * len(out_shape),
        scratch_shapes=[
            pltpu.VMEM((size_x + 2 * WIDTH, size_y, own, depth), jnp.float32),
            pltpu.VMEM((size_x, size_y + 2 * WIDTH, own, depth), jnp.float32),
        ],
        compiler_params=params(),
    )(field, potential, *halos, *before, *extras)


def exchange(to_left, to_right, to_below, to_above):
    def moved(values, axis, by):
        count = lax.axis_size(axis)
        return lax.ppermute(values, axis, [(i, (i + by) % count) for i in range(count)])

    left = moved(to_right, "dx", 1)
    right = moved(to_left, "dx", -1)
    below = moved(to_above, "dy", 1)
    above = moved(to_below, "dy", -1)
    return left, right, below, above


def sum_over_grid(values):
    for axis in ("dx", "dy"):
        count = lax.axis_size(axis)
        sent = jnp.broadcast_to(values[None], (count,) + values.shape)
        values = jnp.sum(lax.all_to_all(sent, axis, 0, 0), axis=0)
    return values


def other_band(values):
    return lax.ppermute(values, "band", [(0, 1), (1, 0)])


def rows_dot(first, second, **kwargs):
    return lax.dot_general(
        first, second, (((1,), (1,)), ((), ())), preferred_element_type=jnp.float32, **kwargs
    )


def shards(orbital_block, potential, resident):
    own_count, size_x, size_y, depth = orbital_block.shape
    cell_count = size_x * size_y * depth
    flat_potential = potential.reshape(size_x * size_y, depth)
    band = lax.axis_index("band")
    half = size_x // 2

    kept = jnp.where(band == 0, resident[:, :half], resident[:, half:])
    given = jnp.where(band == 0, resident[:, half:], resident[:, :half])
    got_resident = other_band(given)

    field, *sent = start(orbital_block)
    fields = [field]
    field, *sent = filter_step(field, flat_potential, exchange(*sent), None, False)
    fields.append(field)
    halos = exchange(*sent)
    field, *sent = filter_step(
        field, flat_potential, halos, fields[0], False, (got_resident,)
    )
    fields.append(field)
    own_resident = resident.reshape(-1, cell_count)
    count = own_resident.shape[0]
    within = rows_dot(own_resident, own_resident)
    across = rows_dot(kept.reshape(count, -1), got_resident.reshape(count, -1))
    overlaps = jnp.stack([within, across])
    halos = exchange(*sent)
    field, *sent = filter_step(field, flat_potential, halos, fields[1], False, (overlaps,))
    overlaps = lax.psum(lax.psum(overlaps, "dx"), "dy")
    overlaps_other = other_band(overlaps)
    (filtered,) = filter_step(field, flat_potential, exchange(*sent), fields[2], True)

    filtered = filtered.reshape(own_count, cell_count)
    rounded = filtered.astype(jnp.bfloat16)
    rest = (filtered - rounded.astype(jnp.float32)).astype(jnp.bfloat16)
    rounded_other = other_band(rounded)
    both = jnp.concatenate([rounded, rounded_other], axis=0)
    parts = jnp.concatenate([both, rest], axis=0)
    local = rows_dot(both, own_resident)
    products = rows_dot(parts, parts)
    n = own_count
    squares_own = products[:n, :n] + products[:n, 2 * n :] + products[2 * n :, :n]
    squares_other = products[:n, n : 2 * n] + products[2 * n :, n : 2 * n]
    squares = jnp.concatenate([squares_own, squares_other], axis=1)
    squares = jnp.pad(squares, ((0, 0), (0, count - 2 * n)))
    summed = sum_over_grid(jnp.concatenate([local, squares], axis=0))
    correlations, squares = summed[: 2 * n], summed[2 * n :, : 2 * n]

    correlations_other = other_band(correlations)
    correlations_rounded = correlations.astype(jnp.bfloat16)
    correction = jnp.dot(correlations_rounded, own_resident, preferred_element_type=jnp.float32)
    got = other_band(correction[n:].astype(jnp.bfloat16))
    projected = filtered - correction[:n] - got.astype(jnp.float32)

    exact = functools.partial(rows_dot, precision=lax.Precision.HIGHEST)
    correlations_other = jnp.concatenate([correlations_other[n:], correlations_other[:n]], axis=0)
    whole = jnp.concatenate([correlations, correlations_other], axis=1)
    whole_rounded = whole.astype(jnp.bfloat16).astype(jnp.float32)
    between = overlaps[1] + overlaps_other[1].T
    overlap = jnp.concatenate(
        [
            jnp.concatenate([overlaps[0], between], axis=1),
            jnp.concatenate([between.T, overlaps_other[0]], axis=1),
        ],
        axis=0,
    )
    weighted = exact(whole_rounded[:n], overlap)
    gram = squares - exact(whole[:n], whole_rounded)
    gram = gram + exact(weighted, whole_rounded)
    gram = gram - exact(whole_rounded[:n], whole)
    turned = jnp.concatenate([gram[:, n:], gram[:, :n]], axis=1)
    gram = jnp.where(band == 0, gram, turned)
    total_cells = cell_count * lax.axis_size("dx") * lax.axis_size("dy")
    return (projected.reshape(orbital_block.shape), gram / total_cells)


def solution(mesh):
    placed = (P("band", "dx", "dy", None), P("dx", "dy", None), P("band", "dx", "dy", None))
    return jax.shard_map(
        shards,
        mesh=mesh,
        in_specs=placed,
        out_specs=(P("band", "dx", "dy", None), P("band", None)),
        check_vma=False,
    )
```

```python
import functools

import jax
import jax.numpy as jnp
import ml_dtypes
import numpy as np
from jax import lax
from jax.experimental import pallas as pl
from jax.experimental.pallas import tpu as pltpu
from jax.sharding import PartitionSpec as P

DEGREE = 4


STENCIL_WEIGHTS = (
    -5369.0 / 1800.0,
    12.0 / 7.0,
    -15.0 / 56.0,
    10.0 / 189.0,
    -1.0 / 112.0,
    2.0 / 1925.0,
    -1.0 / 16632.0,
)
FILTER_CENTER = 23.0
FILTER_HALF = 21.0
WIDTH = 6
SENT = WIDTH + 1
VMEM_BYTES = 24 * 1024 * 1024


def pack_layer(out_ref, at, layer):
    rows = layer.shape[0] * layer.shape[1]
    out_ref[at * rows : (at + 1) * rows, :] = layer.reshape(rows, layer.shape[2]).astype(
        jnp.bfloat16
    )


def pack_messages(parity_ref, field_ref, x_even, x_odd, y_even, y_odd):
    def layer(dim, at):
        return field_ref[at] if dim == 0 else field_ref[:, at]

    for dim, even, odd in ((0, x_even, x_odd), (1, y_even, y_odd)):
        size = field_ref.shape[dim]
        for out_ref, tail in ((even, 1 - parity_ref[dim]), (odd, parity_ref[dim])):
            for at in range(WIDTH):
                pack_layer(out_ref, at, layer(dim, tail * (size - WIDTH) + at))
            nearest = layer(dim, tail * (size - 1))
            pack_layer(out_ref, WIDTH, nearest - nearest.astype(jnp.bfloat16).astype(jnp.float32))


def unpack_messages(parity_ref, halo_x, halo_y, x_even, x_odd, y_even, y_odd):
    for dim, halo, even, odd in ((0, halo_x, x_even, x_odd), (1, halo_y, y_even, y_odd)):
        shape = halo.shape[1:] if dim == 0 else halo.shape[:1] + halo.shape[2:]
        rows = shape[0] * shape[1]
        parity = parity_ref[dim]
        for got, after, near in ((even, 1 - parity, WIDTH - parity), (odd, parity, WIDTH - 1 + parity)):
            def read(at):
                return got[at * rows : (at + 1) * rows, :].astype(jnp.float32).reshape(shape)

            for at in range(WIDTH):
                place = after * WIDTH + at
                if dim == 0:
                    halo[place] = read(at)
                else:
                    halo[:, place] = read(at)
            if dim == 0:
                halo[near] += read(WIDTH)
            else:
                halo[:, near] += read(WIDTH)


def start_kernel(parity_ref, cells_ref, field_ref, *messages):
    size_x, size_y, own = field_ref.shape[:3]
    for x in range(size_x):
        for y in range(size_y):
            rows = pl.ds(x * size_y + y, own, stride=size_x * size_y)
            field_ref[x, y] = cells_ref[rows, :]
    pack_messages(parity_ref, field_ref, *messages)


def step_kernel(scale, has_previous, last, parity_ref, field_ref, potential_ref, band_ref, rest_ref, *refs):
    messages, refs = refs[:4], refs[4:]
    previous_ref = None
    if has_previous:
        previous_ref, refs = refs[0], refs[1:]
    outs, (halo_x, halo_y, total_ref) = refs[:-3], refs[-3:]
    size_x, size_y, own, depth = field_ref.shape
    unpack_messages(parity_ref, halo_x, halo_y, *messages)

    cells = field_ref[...].reshape(size_x * size_y * own, depth)
    high = cells.astype(jnp.bfloat16)
    low = (cells - high.astype(jnp.float32)).astype(jnp.bfloat16)
    along_z = jnp.dot(
        jnp.concatenate([high, low], axis=1), band_ref[...], preferred_element_type=jnp.float32
    ) + jnp.dot(high, rest_ref[...], preferred_element_type=jnp.float32)
    total_ref[...] = along_z.reshape(field_ref.shape)
    weights = [-2.0 * scale * w for w in STENCIL_WEIGHTS]

    @pl.loop(0, size_y)
    def _(y):
        line = [halo_x[k, y] for k in range(WIDTH)]
        line += [field_ref[x, y] for x in range(size_x)]
        line += [halo_x[WIDTH + k, y] for k in range(WIDTH)]
        for x in range(size_x):
            at = WIDTH + x
            total = total_ref[x, y]
            total = total + (scale * potential_ref[pl.ds(x * size_y + y, 1), :]) * line[at]
            if has_previous:
                total = total - previous_ref[x, y]
            for k in range(1, WIDTH + 1):
                total = total + weights[k] * (line[at + k] + line[at - k])
            total_ref[x, y] = total

    @pl.loop(0, size_x)
    def _(x):
        line = [halo_y[x, k] for k in range(WIDTH)]
        line += [field_ref[x, y] for y in range(size_y)]
        line += [halo_y[x, WIDTH + k] for k in range(WIDTH)]
        for y in range(size_y):
            at = WIDTH + y
            total = total_ref[x, y]
            for k in range(1, WIDTH + 1):
                total = total + weights[k] * (line[at + k] + line[at - k])
            if last:
                outs[0][pl.ds(x * size_y + y, own, stride=size_x * size_y), :] = total
            else:
                outs[0][x, y] = total

    if not last:
        pack_messages(parity_ref, *outs)


def message_shapes(size_x, size_y, own, depth):
    to_x = jax.ShapeDtypeStruct((SENT * size_y * own, depth), jnp.bfloat16)
    to_y = jax.ShapeDtypeStruct((SENT * size_x * own, depth), jnp.bfloat16)
    return [to_x, to_x, to_y, to_y]


def params():
    return pltpu.CompilerParams(vmem_limit_bytes=VMEM_BYTES)


def in_vmem(count):
    return [pl.BlockSpec(memory_space=pltpu.VMEM)] * count


def start(parity, orbital_block):
    own, size_x, size_y, depth = orbital_block.shape
    field = jax.ShapeDtypeStruct((size_x, size_y, own, depth), jnp.float32)
    return pl.pallas_call(
        start_kernel,
        out_shape=[field] + message_shapes(size_x, size_y, own, depth),
        in_specs=[pl.BlockSpec(memory_space=pltpu.SMEM)] + in_vmem(1),
        out_specs=in_vmem(5),
        compiler_params=params(),
    )(parity, orbital_block.reshape(own * size_x * size_y, depth))


def depth_matrices(scale, depth):
    weights = [-2.0 * scale * w for w in STENCIL_WEIGHTS]
    away = np.abs(np.arange(depth)[:, None] - np.arange(depth)[None, :])
    matrix = np.zeros((depth, depth), np.float32)
    for k in range(1, WIDTH + 1):
        matrix[away == k] = weights[k]
    matrix[away == 0] = 3.0 * weights[0] - scale * FILTER_CENTER
    high = matrix.astype(ml_dtypes.bfloat16)
    rest = (matrix - high.astype(np.float32)).astype(ml_dtypes.bfloat16)
    return jnp.asarray(np.concatenate([high, high], axis=0)), jnp.asarray(rest)


def filter_step(parity, field, potential, messages, previous, last):
    size_x, size_y, own, depth = field.shape
    scale = (1.0 if previous is None else 2.0) / FILTER_HALF
    if last:
        out_shape = [jax.ShapeDtypeStruct((own * size_x * size_y, depth), jnp.float32)]
    else:
        out_shape = [jax.ShapeDtypeStruct(field.shape, jnp.float32)]
        out_shape += message_shapes(size_x, size_y, own, depth)
    before = [] if previous is None else [previous]
    return pl.pallas_call(
        functools.partial(step_kernel, scale, previous is not None, last),
        out_shape=out_shape,
        in_specs=[pl.BlockSpec(memory_space=pltpu.SMEM)] + in_vmem(8 + len(before)),
        out_specs=in_vmem(len(out_shape)),
        scratch_shapes=[
            pltpu.VMEM((2 * WIDTH, size_y, own, depth), jnp.float32),
            pltpu.VMEM((size_x, 2 * WIDTH, own, depth), jnp.float32),
            pltpu.VMEM(field.shape, jnp.float32),
        ],
        compiler_params=params(),
    )(parity, field, potential, *depth_matrices(scale, depth), *messages, *before)


def swap(x_even, x_odd, y_even, y_odd):
    def swapped(values, axis, first):
        count = lax.axis_size(axis)
        step = lambda i: 1 if (i - first) % 2 == 0 else -1
        return lax.ppermute(values, axis, [(i, (i + step(i)) % count) for i in range(count)])

    return (
        swapped(x_even, "dx", 0),
        swapped(x_odd, "dx", 1),
        swapped(y_even, "dy", 0),
        swapped(y_odd, "dy", 1),
    )


def sum_over_grid(values):
    for axis in ("dx", "dy"):
        count = lax.axis_size(axis)
        sent = jnp.broadcast_to(values[None], (count,) + values.shape)
        values = jnp.sum(lax.all_to_all(sent, axis, 0, 0), axis=0)
    return values


def other_band(values):
    return lax.ppermute(values, "band", [(0, 1), (1, 0)])


def rows_dot(first, second, **kwargs):
    return lax.dot_general(
        first, second, (((1,), (1,)), ((), ())), preferred_element_type=jnp.float32, **kwargs
    )


def shards(orbital_block, potential, resident):
    own_count, size_x, size_y, depth = orbital_block.shape
    cell_count = size_x * size_y * depth
    flat_potential = potential.reshape(size_x * size_y, depth)
    parity = jnp.stack([lax.axis_index("dx") % 2, lax.axis_index("dy") % 2]).astype(jnp.int32)

    field, *messages = start(parity, orbital_block)
    previous = None
    for degree_step in range(DEGREE):
        last = degree_step == DEGREE - 1
        following, *messages = filter_step(
            parity, field, flat_potential, swap(*messages), previous, last
        )
        previous, field = field, following
    filtered = field.reshape(own_count, cell_count)

    rounded = filtered.astype(jnp.bfloat16)
    rounded_other = other_band(rounded)
    own_resident = resident.reshape(-1, cell_count)
    both = jnp.concatenate([rounded, rounded_other], axis=0)
    correlations = sum_over_grid(rows_dot(both, own_resident)).astype(jnp.bfloat16)
    correction = jnp.dot(correlations, own_resident, preferred_element_type=jnp.float32)
    mine, theirs = correction[:own_count], correction[own_count:]
    sent = jnp.concatenate([theirs, mine], axis=0).astype(jnp.bfloat16)
    got = other_band(sent).astype(jnp.float32)
    projected = filtered - mine - got[:own_count]
    projected_other = rounded_other.astype(jnp.float32) - theirs - got[own_count:]
    exact = functools.partial(rows_dot, precision=lax.Precision.HIGHEST)
    partial_own = exact(projected, projected)
    partial_other = exact(projected, projected_other)
    first = jnp.concatenate([partial_own, partial_other], axis=1)
    second = jnp.concatenate([partial_other, partial_own], axis=1)
    partial_gram = jnp.where(lax.axis_index("band") == 0, first, second)
    lanes = 128
    partial_gram = jnp.pad(partial_gram, ((0, 0), (0, lanes - 2 * own_count)))
    total_cells = cell_count * lax.axis_size("dx") * lax.axis_size("dy")
    gram_matrix = sum_over_grid(partial_gram)[:, : 2 * own_count] / total_cells
    return (projected.reshape(orbital_block.shape), gram_matrix)


def solution(mesh):
    placed = (P("band", "dx", "dy", None), P("dx", "dy", None), P("band", "dx", "dy", None))
    return jax.shard_map(
        shards,
        mesh=mesh,
        in_specs=placed,
        out_specs=(P("band", "dx", "dy", None), P("band", None)),
        check_vma=False,
    )
```

```python
import functools

import jax
import jax.numpy as jnp
from jax import lax
from jax.experimental import pallas as pl
from jax.experimental.pallas import tpu as pltpu
from jax.sharding import PartitionSpec as P

DEGREE = 4


STENCIL_WEIGHTS = (
    -5369.0 / 1800.0,
    12.0 / 7.0,
    -15.0 / 56.0,
    10.0 / 189.0,
    -1.0 / 112.0,
    2.0 / 1925.0,
    -1.0 / 16632.0,
)
FILTER_CENTER = 23.0
FILTER_HALF = 21.0
WIDTH = 6
SENT = WIDTH + 1
SENT_SCALE = 1.0 / 64.0
VMEM_BYTES = 8 * 1024 * 1024


def pack_layer(out_ref, at, layer):
    rows = layer.shape[0] * layer.shape[1]
    out_ref[at * rows : (at + 1) * rows, :] = layer.reshape(rows, layer.shape[2]).astype(
        jnp.bfloat16
    )


def pack_messages(parity_ref, field_ref, x_even, x_odd, y_even, y_odd):
    def layer(dim, at):
        return field_ref[at] if dim == 0 else field_ref[:, at]

    for dim, even, odd in ((0, x_even, x_odd), (1, y_even, y_odd)):
        size = field_ref.shape[dim]
        for out_ref, tail in ((even, 1 - parity_ref[dim]), (odd, parity_ref[dim])):
            for at in range(WIDTH):
                pack_layer(out_ref, at, layer(dim, tail * (size - WIDTH) + at))
            nearest = layer(dim, tail * (size - 1))
            pack_layer(out_ref, WIDTH, nearest - nearest.astype(jnp.bfloat16).astype(jnp.float32))


def unpack_messages(parity_ref, halo_x, halo_y, x_even, x_odd, y_even, y_odd):
    for dim, halo, even, odd in ((0, halo_x, x_even, x_odd), (1, halo_y, y_even, y_odd)):
        shape = halo.shape[1:] if dim == 0 else halo.shape[:1] + halo.shape[2:]
        rows = shape[0] * shape[1]
        parity = parity_ref[dim]
        for got, after, near in ((even, 1 - parity, WIDTH - parity), (odd, parity, WIDTH - 1 + parity)):
            def read(at):
                return got[at * rows : (at + 1) * rows, :].astype(jnp.float32).reshape(shape)

            for at in range(WIDTH):
                place = after * WIDTH + at
                if dim == 0:
                    halo[place] = read(at)
                else:
                    halo[:, place] = read(at)
            if dim == 0:
                halo[near] += read(WIDTH)
            else:
                halo[:, near] += read(WIDTH)


def start_kernel(parity_ref, cells_ref, potential_ref, field_ref, kept_ref, band_ref, rest_ref, *messages):
    size_x, size_y, own, depth = field_ref.shape
    kept_ref[...] = potential_ref[...]
    row = lax.broadcasted_iota(jnp.int32, (depth, depth), 0)
    away = jnp.abs(row - lax.broadcasted_iota(jnp.int32, (depth, depth), 1))
    weights = [-2.0 * w / FILTER_HALF for w in STENCIL_WEIGHTS]
    matrix = jnp.where(away == 0, 3.0 * weights[0] - FILTER_CENTER / FILTER_HALF, 0.0)
    for k in range(1, WIDTH + 1):
        matrix = jnp.where(away == k, weights[k], matrix)
    high = matrix.astype(jnp.bfloat16)
    band_ref[:depth, :] = high
    band_ref[depth:, :] = high
    rest_ref[...] = (matrix - high.astype(jnp.float32)).astype(jnp.bfloat16)
    for x in range(size_x):
        for y in range(size_y):
            rows = pl.ds(x * size_y + y, own, stride=size_x * size_y)
            field_ref[x, y] = cells_ref[rows, :]
    pack_messages(parity_ref, field_ref, *messages)


def step_kernel(has_previous, last, parity_ref, field_ref, potential_ref, band_ref, rest_ref, *refs):
    factor = 2.0 if has_previous else 1.0
    scale = factor / FILTER_HALF
    messages, refs = refs[:4], refs[4:]
    previous_ref = None
    if has_previous:
        previous_ref, refs = refs[0], refs[1:]
    outs, (halo_x, halo_y, total_ref) = refs[:-3], refs[-3:]
    size_x, size_y, own, depth = field_ref.shape
    unpack_messages(parity_ref, halo_x, halo_y, *messages)

    cells = field_ref[...].reshape(size_x * size_y * own, depth)
    high = cells.astype(jnp.bfloat16)
    low = (cells - high.astype(jnp.float32)).astype(jnp.bfloat16)
    along_z = jnp.dot(
        jnp.concatenate([high, low], axis=1), band_ref[...], preferred_element_type=jnp.float32
    ) + jnp.dot(high, rest_ref[...], preferred_element_type=jnp.float32)
    total_ref[...] = (factor * along_z).reshape(field_ref.shape)
    weights = [-2.0 * scale * w for w in STENCIL_WEIGHTS]

    @pl.loop(0, size_y)
    def _(y):
        line = [halo_x[k, y] for k in range(WIDTH)]
        line += [field_ref[x, y] for x in range(size_x)]
        line += [halo_x[WIDTH + k, y] for k in range(WIDTH)]
        for x in range(size_x):
            at = WIDTH + x
            total = total_ref[x, y]
            total = total + (scale * potential_ref[pl.ds(x * size_y + y, 1), :]) * line[at]
            if has_previous:
                total = total - previous_ref[x, y]
            for k in range(1, WIDTH + 1):
                total = total + weights[k] * (line[at + k] + line[at - k])
            total_ref[x, y] = total

    @pl.loop(0, size_x)
    def _(x):
        line = [halo_y[x, k] for k in range(WIDTH)]
        line += [field_ref[x, y] for y in range(size_y)]
        line += [halo_y[x, WIDTH + k] for k in range(WIDTH)]
        for y in range(size_y):
            at = WIDTH + y
            total = total_ref[x, y]
            for k in range(1, WIDTH + 1):
                total = total + weights[k] * (line[at + k] + line[at - k])
            if last:
                outs[0][pl.ds(x * size_y + y, own, stride=size_x * size_y), :] = total
            else:
                outs[0][x, y] = total

    if not last:
        pack_messages(parity_ref, *outs)


def message_shapes(size_x, size_y, own, depth):
    to_x = jax.ShapeDtypeStruct((SENT * size_y * own, depth), jnp.bfloat16)
    to_y = jax.ShapeDtypeStruct((SENT * size_x * own, depth), jnp.bfloat16)
    return [to_x, to_x, to_y, to_y]


def params():
    return pltpu.CompilerParams(vmem_limit_bytes=VMEM_BYTES)


def in_vmem(count):
    return [pl.BlockSpec(memory_space=pltpu.VMEM)] * count


def start(parity, orbital_block, potential):
    own, size_x, size_y, depth = orbital_block.shape
    field = jax.ShapeDtypeStruct((size_x, size_y, own, depth), jnp.float32)
    return pl.pallas_call(
        start_kernel,
        out_shape=[
            field,
            jax.ShapeDtypeStruct(potential.shape, jnp.float32),
            jax.ShapeDtypeStruct((2 * depth, depth), jnp.bfloat16),
            jax.ShapeDtypeStruct((depth, depth), jnp.bfloat16),
        ]
        + message_shapes(size_x, size_y, own, depth),
        in_specs=[pl.BlockSpec(memory_space=pltpu.SMEM)] + in_vmem(2),
        out_specs=in_vmem(8),
        compiler_params=params(),
    )(parity, orbital_block.reshape(own * size_x * size_y, depth), potential)


def filter_step(parity, field, fixed, messages, previous, last):
    size_x, size_y, own, depth = field.shape
    if last:
        out_shape = [jax.ShapeDtypeStruct((own * size_x * size_y, depth), jnp.float32)]
    else:
        out_shape = [jax.ShapeDtypeStruct(field.shape, jnp.float32)]
        out_shape += message_shapes(size_x, size_y, own, depth)
    before = [] if previous is None else [previous]
    return pl.pallas_call(
        functools.partial(step_kernel, previous is not None, last),
        out_shape=out_shape,
        in_specs=[pl.BlockSpec(memory_space=pltpu.SMEM)] + in_vmem(8 + len(before)),
        out_specs=in_vmem(len(out_shape)),
        scratch_shapes=[
            pltpu.VMEM((2 * WIDTH, size_y, own, depth), jnp.float32),
            pltpu.VMEM((size_x, 2 * WIDTH, own, depth), jnp.float32),
            pltpu.VMEM(field.shape, jnp.float32),
        ],
        compiler_params=params(),
    )(parity, field, *fixed, *messages, *before)


def swap(x_even, x_odd, y_even, y_odd):
    def swapped(values, axis, first):
        count = lax.axis_size(axis)
        step = lambda i: 1 if (i - first) % 2 == 0 else -1
        return lax.ppermute(values, axis, [(i, (i + step(i)) % count) for i in range(count)])

    return (
        swapped(x_even, "dx", 0),
        swapped(x_odd, "dx", 1),
        swapped(y_even, "dy", 0),
        swapped(y_odd, "dy", 1),
    )


def sum_over_grid(values, sent_type):
    for axis in ("dx", "dy"):
        count = lax.axis_size(axis)
        sent = jnp.broadcast_to(values.astype(sent_type)[None], (count,) + values.shape)
        values = jnp.sum(lax.all_to_all(sent, axis, 0, 0).astype(jnp.float32), axis=0)
    return values


def other_band(values):
    return lax.ppermute(values, "band", [(0, 1), (1, 0)])


def rows_dot(first, second, **kwargs):
    return lax.dot_general(
        first, second, (((1,), (1,)), ((), ())), preferred_element_type=jnp.float32, **kwargs
    )


def shards(orbital_block, potential, resident):
    own_count, size_x, size_y, depth = orbital_block.shape
    cell_count = size_x * size_y * depth
    flat_potential = potential.reshape(size_x * size_y, depth)
    parity = jnp.stack([lax.axis_index("dx") % 2, lax.axis_index("dy") % 2]).astype(jnp.int32)

    field, *rest = start(parity, orbital_block, flat_potential)
    fixed, messages = rest[:3], rest[3:]
    previous = None
    for degree_step in range(DEGREE):
        last = degree_step == DEGREE - 1
        following, *messages = filter_step(
            parity, field, fixed, swap(*messages), previous, last
        )
        previous, field = field, following
    filtered = field.reshape(own_count, cell_count)

    rounded = filtered.astype(jnp.bfloat16)
    rounded_other = other_band(rounded)
    own_resident = resident.reshape(-1, cell_count)
    both = jnp.concatenate([rounded, rounded_other], axis=0)
    local = rows_dot(both, own_resident) * SENT_SCALE
    correlations = (sum_over_grid(local, jnp.float16) / SENT_SCALE).astype(jnp.bfloat16)
    correction = jnp.dot(correlations, own_resident, preferred_element_type=jnp.float32)
    mine, theirs = correction[:own_count], correction[own_count:]
    sent = jnp.concatenate([theirs, mine], axis=0).astype(jnp.bfloat16)
    got = other_band(sent).astype(jnp.float32)
    projected = filtered - mine - got[:own_count]
    projected_other = rounded_other.astype(jnp.float32) - theirs - got[own_count:]
    exact = functools.partial(rows_dot, precision=lax.Precision.HIGHEST)
    partial_gram = exact(projected, jnp.concatenate([projected, projected_other], axis=0))
    turned = jnp.roll(partial_gram, own_count, axis=1)
    partial_gram = jnp.where(lax.axis_index("band") == 0, partial_gram, turned)
    lanes = 128
    partial_gram = jnp.pad(partial_gram, ((0, 0), (0, lanes - 2 * own_count)))
    total_cells = cell_count * lax.axis_size("dx") * lax.axis_size("dy")
    gram_matrix = sum_over_grid(partial_gram, jnp.float32)[:, : 2 * own_count] / total_cells
    return (projected.reshape(orbital_block.shape), gram_matrix)


def solution(mesh):
    placed = (P("band", "dx", "dy", None), P("dx", "dy", None), P("band", "dx", "dy", None))
    return jax.shard_map(
        shards,
        mesh=mesh,
        in_specs=placed,
        out_specs=(P("band", "dx", "dy", None), P("band", None)),
        check_vma=False,
    )
```

```python
import functools

import jax
import jax.numpy as jnp
from jax import lax
from jax.experimental import pallas as pl
from jax.experimental.pallas import tpu as pltpu
from jax.sharding import PartitionSpec as P

DEGREE = 4


STENCIL_WEIGHTS = (
    -5369.0 / 1800.0,
    12.0 / 7.0,
    -15.0 / 56.0,
    10.0 / 189.0,
    -1.0 / 112.0,
    2.0 / 1925.0,
    -1.0 / 16632.0,
)
FILTER_CENTER = 23.0
FILTER_HALF = 21.0
WIDTH = 6
SENT = WIDTH + 1
SENT_SCALE = 1.0 / 64.0
VMEM_BYTES = 8 * 1024 * 1024


def pack_layer(out_ref, at, layer):
    rows = layer.shape[0] * layer.shape[1]
    out_ref[at * rows : (at + 1) * rows, :] = layer.reshape(rows, layer.shape[2]).astype(
        jnp.bfloat16
    )


def pack_messages(parity_ref, field_ref, y_odd, x_even, x_odd, y_even):
    def layer(dim, at):
        return field_ref[at] if dim == 0 else field_ref[:, at]

    for dim, even, odd in ((0, x_even, x_odd), (1, y_even, y_odd)):
        size = field_ref.shape[dim]
        for out_ref, tail in ((even, 1 - parity_ref[dim]), (odd, parity_ref[dim])):
            for at in range(WIDTH):
                pack_layer(out_ref, at, layer(dim, tail * (size - WIDTH) + at))
            nearest = layer(dim, tail * (size - 1))
            pack_layer(out_ref, WIDTH, nearest - nearest.astype(jnp.bfloat16).astype(jnp.float32))
            used = SENT * nearest.shape[0] * nearest.shape[1]
            if used < out_ref.shape[0]:
                rows = out_ref.shape[0] - used
                out_ref[used:, :] = jnp.zeros((rows, out_ref.shape[1]), jnp.bfloat16)


def unpack_messages(parity_ref, halo_x, halo_y, y_odd, x_even, x_odd, y_even):
    for dim, halo, even, odd in ((0, halo_x, x_even, x_odd), (1, halo_y, y_even, y_odd)):
        shape = halo.shape[1:] if dim == 0 else halo.shape[:1] + halo.shape[2:]
        rows = shape[0] * shape[1]
        parity = parity_ref[dim]
        for got, after, near in ((even, 1 - parity, WIDTH - parity), (odd, parity, WIDTH - 1 + parity)):
            def read(at):
                return got[at * rows : (at + 1) * rows, :].astype(jnp.float32).reshape(shape)

            for at in range(WIDTH):
                place = after * WIDTH + at
                if dim == 0:
                    halo[place] = read(at)
                else:
                    halo[:, place] = read(at)
            if dim == 0:
                halo[near] += read(WIDTH)
            else:
                halo[:, near] += read(WIDTH)


def start_kernel(parity_ref, cells_ref, potential_ref, field_ref, kept_ref, band_ref, rest_ref, *messages):
    size_x, size_y, own, depth = field_ref.shape
    kept_ref[...] = potential_ref[...]
    row = lax.broadcasted_iota(jnp.int32, (depth, depth), 0)
    away = jnp.abs(row - lax.broadcasted_iota(jnp.int32, (depth, depth), 1))
    weights = [-2.0 * w / FILTER_HALF for w in STENCIL_WEIGHTS]
    matrix = jnp.where(away == 0, 3.0 * weights[0] - FILTER_CENTER / FILTER_HALF, 0.0)
    for k in range(1, WIDTH + 1):
        matrix = jnp.where(away == k, weights[k], matrix)
    high = matrix.astype(jnp.bfloat16)
    band_ref[:depth, :] = high
    band_ref[depth:, :] = high
    rest_ref[...] = (matrix - high.astype(jnp.float32)).astype(jnp.bfloat16)
    for x in range(size_x):
        for y in range(size_y):
            rows = pl.ds(x * size_y + y, own, stride=size_x * size_y)
            field_ref[x, y] = cells_ref[rows, :]
    pack_messages(parity_ref, field_ref, *messages)


def step_kernel(has_previous, last, parity_ref, field_ref, potential_ref, band_ref, rest_ref, *refs):
    factor = 2.0 if has_previous else 1.0
    scale = factor / FILTER_HALF
    messages, refs = refs[:4], refs[4:]
    previous_ref = None
    if has_previous:
        previous_ref, refs = refs[0], refs[1:]
    outs, (halo_x, halo_y, total_ref) = refs[:-3], refs[-3:]
    size_x, size_y, own, depth = field_ref.shape
    unpack_messages(parity_ref, halo_x, halo_y, *messages)

    cells = field_ref[...].reshape(size_x * size_y * own, depth)
    high = cells.astype(jnp.bfloat16)
    low = (cells - high.astype(jnp.float32)).astype(jnp.bfloat16)
    along_z = jnp.dot(
        jnp.concatenate([high, low], axis=1), band_ref[...], preferred_element_type=jnp.float32
    ) + jnp.dot(high, rest_ref[...], preferred_element_type=jnp.float32)
    total_ref[...] = (factor * along_z).reshape(field_ref.shape)
    weights = [-2.0 * scale * w for w in STENCIL_WEIGHTS]

    @pl.loop(0, size_y)
    def _(y):
        line = [halo_x[k, y] for k in range(WIDTH)]
        line += [field_ref[x, y] for x in range(size_x)]
        line += [halo_x[WIDTH + k, y] for k in range(WIDTH)]
        for x in range(size_x):
            at = WIDTH + x
            total = total_ref[x, y]
            total = total + (scale * potential_ref[pl.ds(x * size_y + y, 1), :]) * line[at]
            if has_previous:
                total = total - previous_ref[x, y]
            for k in range(1, WIDTH + 1):
                total = total + weights[k] * (line[at + k] + line[at - k])
            total_ref[x, y] = total

    @pl.loop(0, size_x)
    def _(x):
        line = [halo_y[x, k] for k in range(WIDTH)]
        line += [field_ref[x, y] for y in range(size_y)]
        line += [halo_y[x, WIDTH + k] for k in range(WIDTH)]
        for y in range(size_y):
            at = WIDTH + y
            total = total_ref[x, y]
            for k in range(1, WIDTH + 1):
                total = total + weights[k] * (line[at + k] + line[at - k])
            if last:
                outs[0][pl.ds(x * size_y + y, own, stride=size_x * size_y), :] = total
            else:
                outs[0][x, y] = total

    if not last:
        pack_messages(parity_ref, *outs)


def message_shapes(size_x, size_y, own, depth):
    rows = SENT * max(size_x, size_y) * own
    return [jax.ShapeDtypeStruct((rows, depth), jnp.bfloat16)] * 4


def params():
    return pltpu.CompilerParams(vmem_limit_bytes=VMEM_BYTES)


def in_vmem(count):
    return [pl.BlockSpec(memory_space=pltpu.VMEM)] * count


def start(parity, orbital_block, potential):
    own, size_x, size_y, depth = orbital_block.shape
    field = jax.ShapeDtypeStruct((size_x, size_y, own, depth), jnp.float32)
    return pl.pallas_call(
        start_kernel,
        out_shape=[
            field,
            jax.ShapeDtypeStruct(potential.shape, jnp.float32),
            jax.ShapeDtypeStruct((2 * depth, depth), jnp.bfloat16),
            jax.ShapeDtypeStruct((depth, depth), jnp.bfloat16),
        ]
        + message_shapes(size_x, size_y, own, depth),
        in_specs=[pl.BlockSpec(memory_space=pltpu.SMEM)] + in_vmem(2),
        out_specs=in_vmem(8),
        compiler_params=params(),
    )(parity, orbital_block.reshape(own * size_x * size_y, depth), potential)


def filter_step(parity, field, fixed, messages, previous, last):
    size_x, size_y, own, depth = field.shape
    if last:
        out_shape = [jax.ShapeDtypeStruct((own * size_x * size_y, depth), jnp.float32)]
    else:
        out_shape = [jax.ShapeDtypeStruct(field.shape, jnp.float32)]
        out_shape += message_shapes(size_x, size_y, own, depth)
    before = [] if previous is None else [previous]
    return pl.pallas_call(
        functools.partial(step_kernel, previous is not None, last),
        out_shape=out_shape,
        in_specs=[pl.BlockSpec(memory_space=pltpu.SMEM)] + in_vmem(8 + len(before)),
        out_specs=in_vmem(len(out_shape)),
        scratch_shapes=[
            pltpu.VMEM((2 * WIDTH, size_y, own, depth), jnp.float32),
            pltpu.VMEM((size_x, 2 * WIDTH, own, depth), jnp.float32),
            pltpu.VMEM(field.shape, jnp.float32),
        ],
        compiler_params=params(),
    )(parity, field, *fixed, *messages, *before)


def swap(y_odd, x_even, x_odd, y_even):
    def swapped(values, axis, first):
        count = lax.axis_size(axis)
        step = lambda i: 1 if (i - first) % 2 == 0 else -1
        return lax.ppermute(values, axis, [(i, (i + step(i)) % count) for i in range(count)])

    return (
        swapped(y_odd, "dy", 1),
        swapped(x_even, "dx", 0),
        swapped(x_odd, "dx", 1),
        swapped(y_even, "dy", 0),
    )


def sum_over_grid(values, sent_type):
    for axis in ("dx", "dy"):
        count = lax.axis_size(axis)
        sent = jnp.broadcast_to(values.astype(sent_type)[None], (count,) + values.shape)
        values = jnp.sum(lax.all_to_all(sent, axis, 0, 0).astype(jnp.float32), axis=0)
    return values


def other_band(values):
    return lax.ppermute(values, "band", [(0, 1), (1, 0)])


def rows_dot(first, second, **kwargs):
    return lax.dot_general(
        first, second, (((1,), (1,)), ((), ())), preferred_element_type=jnp.float32, **kwargs
    )


def shards(orbital_block, potential, resident):
    own_count, size_x, size_y, depth = orbital_block.shape
    cell_count = size_x * size_y * depth
    flat_potential = potential.reshape(size_x * size_y, depth)
    parity = jnp.stack([lax.axis_index("dx") % 2, lax.axis_index("dy") % 2]).astype(jnp.int32)

    field, *rest = start(parity, orbital_block, flat_potential)
    fixed, messages = rest[:3], rest[3:]
    previous = None
    for degree_step in range(DEGREE):
        last = degree_step == DEGREE - 1
        following, *messages = filter_step(
            parity, field, fixed, swap(*messages), previous, last
        )
        previous, field = field, following
    filtered = field.reshape(own_count, cell_count)

    rounded = filtered.astype(jnp.bfloat16)
    rounded_other = other_band(rounded)
    own_resident = resident.reshape(-1, cell_count)
    local_own = rows_dot(rounded, own_resident)
    local_other = rows_dot(rounded_other, own_resident)
    local = jnp.concatenate([local_own, local_other], axis=0) * SENT_SCALE
    correlations = (sum_over_grid(local, jnp.float16) / SENT_SCALE).astype(jnp.bfloat16)
    correction = jnp.dot(correlations, own_resident, preferred_element_type=jnp.float32)
    mine, theirs = correction[:own_count], correction[own_count:]
    sent = jnp.concatenate([theirs, mine], axis=0).astype(jnp.bfloat16)
    got = other_band(sent).astype(jnp.float32)
    projected = filtered - mine - got[:own_count]
    projected_other = rounded_other.astype(jnp.float32) - theirs - got[own_count:]
    exact = functools.partial(rows_dot, precision=lax.Precision.HIGHEST)
    partial_gram = exact(projected, jnp.concatenate([projected, projected_other], axis=0))
    turned = jnp.roll(partial_gram, own_count, axis=1)
    partial_gram = jnp.where(lax.axis_index("band") == 0, partial_gram, turned)
    lanes = 128
    partial_gram = jnp.pad(partial_gram, ((0, 0), (0, lanes - 2 * own_count)))
    total_cells = cell_count * lax.axis_size("dx") * lax.axis_size("dy")
    gram_matrix = sum_over_grid(partial_gram, jnp.float32)[:, : 2 * own_count] / total_cells
    return (projected.reshape(orbital_block.shape), gram_matrix)


def solution(mesh):
    placed = (P("band", "dx", "dy", None), P("dx", "dy", None), P("band", "dx", "dy", None))
    return jax.shard_map(
        shards,
        mesh=mesh,
        in_specs=placed,
        out_specs=(P("band", "dx", "dy", None), P("band", None)),
        check_vma=False,
    )
```

```python
import functools

import jax
import jax.numpy as jnp
from jax import lax
from jax.experimental import pallas as pl
from jax.experimental.pallas import tpu as pltpu
from jax.sharding import PartitionSpec as P

DEGREE = 4


STENCIL_WEIGHTS = (
    -5369.0 / 1800.0,
    12.0 / 7.0,
    -15.0 / 56.0,
    10.0 / 189.0,
    -1.0 / 112.0,
    2.0 / 1925.0,
    -1.0 / 16632.0,
)
FILTER_CENTER = 23.0
FILTER_HALF = 21.0
WIDTH = 6
SENT = WIDTH + 1
SENT_SCALE = 1.0 / 64.0
VMEM_BYTES = 8 * 1024 * 1024


def pack_layer(out_ref, at, layer):
    rows = layer.shape[0] * layer.shape[1]
    out_ref[at * rows : (at + 1) * rows, :] = layer.reshape(rows, layer.shape[2]).astype(
        jnp.bfloat16
    )


def pack_messages(parity_ref, field_ref, y_odd, x_even, x_odd, y_even):
    def layer(dim, at):
        return field_ref[at] if dim == 0 else field_ref[:, at]

    for dim, even, odd in ((0, x_even, x_odd), (1, y_even, y_odd)):
        size = field_ref.shape[dim]
        for out_ref, tail in ((even, 1 - parity_ref[dim]), (odd, parity_ref[dim])):
            for at in range(WIDTH):
                pack_layer(out_ref, at, layer(dim, tail * (size - WIDTH) + at))
            nearest = layer(dim, tail * (size - 1))
            pack_layer(out_ref, WIDTH, nearest - nearest.astype(jnp.bfloat16).astype(jnp.float32))
            used = SENT * nearest.shape[0] * nearest.shape[1]
            if used < out_ref.shape[0]:
                rows = out_ref.shape[0] - used
                out_ref[used:, :] = jnp.zeros((rows, out_ref.shape[1]), jnp.bfloat16)


def unpack_messages(parity_ref, halo_x, halo_y, y_odd, x_even, x_odd, y_even):
    for dim, halo, even, odd in ((0, halo_x, x_even, x_odd), (1, halo_y, y_even, y_odd)):
        shape = halo.shape[1:] if dim == 0 else halo.shape[:1] + halo.shape[2:]
        rows = shape[0] * shape[1]
        parity = parity_ref[dim]
        for got, after, near in ((even, 1 - parity, WIDTH - parity), (odd, parity, WIDTH - 1 + parity)):
            def read(at):
                return got[at * rows : (at + 1) * rows, :].astype(jnp.float32).reshape(shape)

            for at in range(WIDTH):
                place = after * WIDTH + at
                if dim == 0:
                    halo[place] = read(at)
                else:
                    halo[:, place] = read(at)
            if dim == 0:
                halo[near] += read(WIDTH)
            else:
                halo[:, near] += read(WIDTH)


def start_kernel(parity_ref, cells_ref, potential_ref, field_ref, kept_ref, band_ref, rest_ref, *messages):
    size_x, size_y, own, depth = field_ref.shape
    kept_ref[...] = potential_ref[...]
    row = lax.broadcasted_iota(jnp.int32, (depth, depth), 0)
    away = jnp.abs(row - lax.broadcasted_iota(jnp.int32, (depth, depth), 1))
    weights = [-2.0 * w / FILTER_HALF for w in STENCIL_WEIGHTS]
    matrix = jnp.where(away == 0, 3.0 * weights[0] - FILTER_CENTER / FILTER_HALF, 0.0)
    for k in range(1, WIDTH + 1):
        matrix = jnp.where(away == k, weights[k], matrix)
    high = matrix.astype(jnp.bfloat16)
    band_ref[:depth, :] = high
    band_ref[depth:, :] = high
    rest_ref[...] = (matrix - high.astype(jnp.float32)).astype(jnp.bfloat16)
    for x in range(size_x):
        for y in range(size_y):
            rows = pl.ds(x * size_y + y, own, stride=size_x * size_y)
            field_ref[x, y] = cells_ref[rows, :]
    pack_messages(parity_ref, field_ref, *messages)


def inner_kernel(has_previous, field_ref, potential_ref, band_ref, rest_ref, *refs):
    previous_ref = refs[0] if has_previous else None
    total_ref = refs[-1]
    factor = 2.0 if has_previous else 1.0
    scale = factor / FILTER_HALF
    size_x, size_y, own, depth = field_ref.shape

    cells = field_ref[...].reshape(size_x * size_y * own, depth)
    high = cells.astype(jnp.bfloat16)
    low = (cells - high.astype(jnp.float32)).astype(jnp.bfloat16)
    along_z = jnp.dot(
        jnp.concatenate([high, low], axis=1), band_ref[...], preferred_element_type=jnp.float32
    ) + jnp.dot(high, rest_ref[...], preferred_element_type=jnp.float32)
    total_ref[...] = (factor * along_z).reshape(field_ref.shape)
    weights = [-2.0 * scale * w for w in STENCIL_WEIGHTS]

    def inside(total, line, at):
        for k in range(1, WIDTH + 1):
            near = [line[i] for i in (at - k, at + k) if 0 <= i < len(line)]
            if near:
                total = total + weights[k] * sum(near[1:], near[0])
        return total

    @pl.loop(0, size_y)
    def _(y):
        line = [field_ref[x, y] for x in range(size_x)]
        for x in range(size_x):
            total = total_ref[x, y]
            total = total + (scale * potential_ref[pl.ds(x * size_y + y, 1), :]) * line[x]
            if has_previous:
                total = total - previous_ref[x, y]
            total_ref[x, y] = inside(total, line, x)

    @pl.loop(0, size_x)
    def _(x):
        line = [field_ref[x, y] for y in range(size_y)]
        for y in range(size_y):
            total_ref[x, y] = inside(total_ref[x, y], line, y)


def outer_kernel(factor, last, parity_ref, inner_ref, *refs):
    messages, outs, (halo_x, halo_y, total_ref) = refs[:4], refs[4:-3], refs[-3:]
    size_x, size_y, own, depth = inner_ref.shape
    unpack_messages(parity_ref, halo_x, halo_y, *messages)
    weights = [-2.0 * factor / FILTER_HALF * w for w in STENCIL_WEIGHTS]

    def outside(total, line, at, size):
        for k in range(1, WIDTH + 1):
            if at - k < 0:
                total = total + weights[k] * line[WIDTH + at - k]
            if at + k >= size:
                total = total + weights[k] * line[WIDTH + at + k - size]
        return total

    @pl.loop(0, size_y)
    def _(y):
        line = [halo_x[k, y] for k in range(2 * WIDTH)]
        for x in range(size_x):
            total_ref[x, y] = outside(inner_ref[x, y], line, x, size_x)

    @pl.loop(0, size_x)
    def _(x):
        line = [halo_y[x, k] for k in range(2 * WIDTH)]
        for y in range(size_y):
            total = outside(total_ref[x, y], line, y, size_y)
            if last:
                place = pl.multiple_of((x * size_y + y) * depth, depth)
                outs[0][:, pl.ds(place, depth)] = total
            else:
                outs[0][x, y] = total

    if not last:
        pack_messages(parity_ref, *outs)


def message_shapes(size_x, size_y, own, depth):
    rows = SENT * max(size_x, size_y) * own
    return [jax.ShapeDtypeStruct((rows, depth), jnp.bfloat16)] * 4


def params():
    return pltpu.CompilerParams(vmem_limit_bytes=VMEM_BYTES)


def in_vmem(count):
    return [pl.BlockSpec(memory_space=pltpu.VMEM)] * count


def start(parity, orbital_block, potential):
    own, size_x, size_y, depth = orbital_block.shape
    field = jax.ShapeDtypeStruct((size_x, size_y, own, depth), jnp.float32)
    return pl.pallas_call(
        start_kernel,
        out_shape=[
            field,
            jax.ShapeDtypeStruct(potential.shape, jnp.float32),
            jax.ShapeDtypeStruct((2 * depth, depth), jnp.bfloat16),
            jax.ShapeDtypeStruct((depth, depth), jnp.bfloat16),
        ]
        + message_shapes(size_x, size_y, own, depth),
        in_specs=[pl.BlockSpec(memory_space=pltpu.SMEM)] + in_vmem(2),
        out_specs=in_vmem(8),
        compiler_params=params(),
    )(parity, orbital_block.reshape(own * size_x * size_y, depth), potential)


def filter_step(parity, field, fixed, messages, previous, last):
    size_x, size_y, own, depth = field.shape
    field_shape = jax.ShapeDtypeStruct(field.shape, jnp.float32)
    before = [] if previous is None else [previous]
    inner = pl.pallas_call(
        functools.partial(inner_kernel, previous is not None),
        out_shape=field_shape,
        in_specs=in_vmem(4 + len(before)),
        out_specs=in_vmem(1)[0],
        compiler_params=params(),
        cost_estimate=pl.CostEstimate(
            flops=6 * field.size * depth, bytes_accessed=12 * field.size, transcendentals=0
        ),
    )(field, *fixed, *before)
    if last:
        out_shape = [jax.ShapeDtypeStruct((own, size_x * size_y * depth), jnp.float32)]
    else:
        out_shape = [field_shape] + message_shapes(size_x, size_y, own, depth)
    return pl.pallas_call(
        functools.partial(outer_kernel, 1.0 if previous is None else 2.0, last),
        out_shape=out_shape,
        in_specs=[pl.BlockSpec(memory_space=pltpu.SMEM)] + in_vmem(5),
        out_specs=in_vmem(len(out_shape)),
        scratch_shapes=[
            pltpu.VMEM((2 * WIDTH, size_y, own, depth), jnp.float32),
            pltpu.VMEM((size_x, 2 * WIDTH, own, depth), jnp.float32),
            pltpu.VMEM(field.shape, jnp.float32),
        ],
        compiler_params=params(),
    )(parity, inner, *messages)


def swap(y_odd, x_even, x_odd, y_even):
    def swapped(values, axis, first):
        count = lax.axis_size(axis)
        step = lambda i: 1 if (i - first) % 2 == 0 else -1
        return lax.ppermute(values, axis, [(i, (i + step(i)) % count) for i in range(count)])

    return (
        swapped(y_odd, "dy", 1),
        swapped(x_even, "dx", 0),
        swapped(x_odd, "dx", 1),
        swapped(y_even, "dy", 0),
    )


def sum_over_grid(values, sent_type):
    for axis in ("dx", "dy"):
        count = lax.axis_size(axis)
        sent = jnp.broadcast_to(values.astype(sent_type)[None], (count,) + values.shape)
        values = jnp.sum(lax.all_to_all(sent, axis, 0, 0).astype(jnp.float32), axis=0)
    return values


def other_band(values):
    return lax.ppermute(values, "band", [(0, 1), (1, 0)])


def rows_dot(first, second, **kwargs):
    return lax.dot_general(
        first, second, (((1,), (1,)), ((), ())), preferred_element_type=jnp.float32, **kwargs
    )


def shards(orbital_block, potential, resident):
    own_count, size_x, size_y, depth = orbital_block.shape
    cell_count = size_x * size_y * depth
    flat_potential = potential.reshape(size_x * size_y, depth)
    parity = jnp.stack([lax.axis_index("dx") % 2, lax.axis_index("dy") % 2]).astype(jnp.int32)

    field, *rest = start(parity, orbital_block, flat_potential)
    fixed, messages = rest[:3], rest[3:]
    previous = None
    for degree_step in range(DEGREE):
        last = degree_step == DEGREE - 1
        following, *messages = filter_step(
            parity, field, fixed, swap(*messages), previous, last
        )
        previous, field = field, following
    filtered = field

    rounded = filtered.astype(jnp.bfloat16)
    rounded_other = other_band(rounded)
    own_resident = resident.reshape(-1, cell_count)
    local_own = rows_dot(rounded, own_resident)
    local_other = rows_dot(rounded_other, own_resident)
    local = jnp.concatenate([local_own, local_other], axis=0) * SENT_SCALE
    correlations = (sum_over_grid(local, jnp.float16) / SENT_SCALE).astype(jnp.bfloat16)
    correction = jnp.dot(correlations, own_resident, preferred_element_type=jnp.float32)
    mine, theirs = correction[:own_count], correction[own_count:]
    sent = jnp.concatenate([theirs, mine], axis=0).astype(jnp.bfloat16)
    got = other_band(sent).astype(jnp.float32)
    projected = filtered - mine - got[:own_count]
    projected_other = rounded_other.astype(jnp.float32) - theirs - got[own_count:]
    exact = functools.partial(rows_dot, precision=lax.Precision.HIGHEST)
    partial_gram = exact(projected, jnp.concatenate([projected, projected_other], axis=0))
    turned = jnp.roll(partial_gram, own_count, axis=1)
    partial_gram = jnp.where(lax.axis_index("band") == 0, partial_gram, turned)
    lanes = 128
    partial_gram = jnp.pad(partial_gram, ((0, 0), (0, lanes - 2 * own_count)))
    total_cells = cell_count * lax.axis_size("dx") * lax.axis_size("dy")
    gram_matrix = sum_over_grid(partial_gram, jnp.float32)[:, : 2 * own_count] / total_cells
    return (projected.reshape(orbital_block.shape), gram_matrix)


def solution(mesh):
    placed = (P("band", "dx", "dy", None), P("dx", "dy", None), P("band", "dx", "dy", None))
    return jax.shard_map(
        shards,
        mesh=mesh,
        in_specs=placed,
        out_specs=(P("band", "dx", "dy", None), P("band", None)),
        check_vma=False,
    )
```

```python
import functools

import jax
import jax.numpy as jnp
from jax import lax
from jax.experimental import pallas as pl
from jax.experimental.pallas import tpu as pltpu
from jax.sharding import PartitionSpec as P

DEGREE = 4


STENCIL_WEIGHTS = (
    -5369.0 / 1800.0,
    12.0 / 7.0,
    -15.0 / 56.0,
    10.0 / 189.0,
    -1.0 / 112.0,
    2.0 / 1925.0,
    -1.0 / 16632.0,
)
FILTER_CENTER = 23.0
FILTER_HALF = 21.0
WIDTH = 6
SENT = WIDTH + 1
SENT_SCALE = 1.0 / 64.0
VMEM_BYTES = 8 * 1024 * 1024


def pack_layer(out_ref, at, layer):
    rows = layer.shape[0] * layer.shape[1]
    out_ref[at * rows : (at + 1) * rows, :] = layer.reshape(rows, layer.shape[2]).astype(
        jnp.bfloat16
    )


def pack_messages(parity_ref, field_ref, y_odd, x_even, x_odd, y_even):
    def layer(dim, at):
        return field_ref[at] if dim == 0 else field_ref[:, at]

    for dim, even, odd in ((0, x_even, x_odd), (1, y_even, y_odd)):
        size = field_ref.shape[dim]
        for out_ref, tail in ((even, 1 - parity_ref[dim]), (odd, parity_ref[dim])):
            for at in range(WIDTH):
                pack_layer(out_ref, at, layer(dim, tail * (size - WIDTH) + at))
            nearest = layer(dim, tail * (size - 1))
            pack_layer(out_ref, WIDTH, nearest - nearest.astype(jnp.bfloat16).astype(jnp.float32))
            used = SENT * nearest.shape[0] * nearest.shape[1]
            if used < out_ref.shape[0]:
                rows = out_ref.shape[0] - used
                out_ref[used:, :] = jnp.zeros((rows, out_ref.shape[1]), jnp.bfloat16)


def unpack_messages(parity_ref, halo_x, halo_y, y_odd, x_even, x_odd, y_even):
    for dim, halo, even, odd in ((0, halo_x, x_even, x_odd), (1, halo_y, y_even, y_odd)):
        shape = halo.shape[1:] if dim == 0 else halo.shape[:1] + halo.shape[2:]
        rows = shape[0] * shape[1]
        parity = parity_ref[dim]
        for got, after, near in ((even, 1 - parity, WIDTH - parity), (odd, parity, WIDTH - 1 + parity)):
            def read(at):
                return got[at * rows : (at + 1) * rows, :].astype(jnp.float32).reshape(shape)

            for at in range(WIDTH):
                place = after * WIDTH + at
                if dim == 0:
                    halo[place] = read(at)
                else:
                    halo[:, place] = read(at)
            if dim == 0:
                halo[near] += read(WIDTH)
            else:
                halo[:, near] += read(WIDTH)


def start_kernel(parity_ref, cells_ref, field_ref, *messages):
    size_x, size_y, own = field_ref.shape[:3]
    for x in range(size_x):
        for y in range(size_y):
            rows = pl.ds(x * size_y + y, own, stride=size_x * size_y)
            field_ref[x, y] = cells_ref[rows, :]
    pack_messages(parity_ref, field_ref, *messages)


def fixed_kernel(potential_ref, kept_ref, band_ref, rest_ref):
    depth = rest_ref.shape[0]
    kept_ref[...] = potential_ref[...]
    row = lax.broadcasted_iota(jnp.int32, (depth, depth), 0)
    away = jnp.abs(row - lax.broadcasted_iota(jnp.int32, (depth, depth), 1))
    weights = [-2.0 * w / FILTER_HALF for w in STENCIL_WEIGHTS]
    matrix = jnp.where(away == 0, 3.0 * weights[0] - FILTER_CENTER / FILTER_HALF, 0.0)
    for k in range(1, WIDTH + 1):
        matrix = jnp.where(away == k, weights[k], matrix)
    high = matrix.astype(jnp.bfloat16)
    band_ref[:depth, :] = high
    band_ref[depth:, :] = high
    rest_ref[...] = (matrix - high.astype(jnp.float32)).astype(jnp.bfloat16)


def inner_kernel(has_previous, field_ref, potential_ref, band_ref, rest_ref, *refs):
    previous_ref = refs[0] if has_previous else None
    total_ref = refs[-1]
    factor = 2.0 if has_previous else 1.0
    scale = factor / FILTER_HALF
    size_x, size_y, own, depth = field_ref.shape

    cells = field_ref[...].reshape(size_x * size_y * own, depth)
    high = cells.astype(jnp.bfloat16)
    low = (cells - high.astype(jnp.float32)).astype(jnp.bfloat16)
    along_z = jnp.dot(
        jnp.concatenate([high, low], axis=1), band_ref[...], preferred_element_type=jnp.float32
    ) + jnp.dot(high, rest_ref[...], preferred_element_type=jnp.float32)
    total_ref[...] = (factor * along_z).reshape(field_ref.shape)
    weights = [-2.0 * scale * w for w in STENCIL_WEIGHTS]

    def inside(total, line, at):
        for k in range(1, WIDTH + 1):
            near = [line[i] for i in (at - k, at + k) if 0 <= i < len(line)]
            if near:
                total = total + weights[k] * sum(near[1:], near[0])
        return total

    @pl.loop(0, size_y)
    def _(y):
        line = [field_ref[x, y] for x in range(size_x)]
        for x in range(size_x):
            total = total_ref[x, y]
            total = total + (scale * potential_ref[pl.ds(x * size_y + y, 1), :]) * line[x]
            if has_previous:
                total = total - previous_ref[x, y]
            total_ref[x, y] = inside(total, line, x)

    @pl.loop(0, size_x)
    def _(x):
        line = [field_ref[x, y] for y in range(size_y)]
        for y in range(size_y):
            total_ref[x, y] = inside(total_ref[x, y], line, y)


def outer_kernel(factor, last, parity_ref, inner_ref, *refs):
    messages, outs, (halo_x, halo_y, total_ref) = refs[:4], refs[4:-3], refs[-3:]
    size_x, size_y, own, depth = inner_ref.shape
    unpack_messages(parity_ref, halo_x, halo_y, *messages)
    weights = [-2.0 * factor / FILTER_HALF * w for w in STENCIL_WEIGHTS]

    def outside(total, line, at, size):
        for k in range(1, WIDTH + 1):
            if at - k < 0:
                total = total + weights[k] * line[WIDTH + at - k]
            if at + k >= size:
                total = total + weights[k] * line[WIDTH + at + k - size]
        return total

    @pl.loop(0, size_y)
    def _(y):
        line = [halo_x[k, y] for k in range(2 * WIDTH)]
        for x in range(size_x):
            total_ref[x, y] = outside(inner_ref[x, y], line, x, size_x)

    @pl.loop(0, size_x)
    def _(x):
        line = [halo_y[x, k] for k in range(2 * WIDTH)]
        for y in range(size_y):
            total = outside(total_ref[x, y], line, y, size_y)
            if last:
                place = pl.multiple_of((x * size_y + y) * depth, depth)
                outs[0][:, pl.ds(place, depth)] = total
            else:
                outs[0][x, y] = total

    if not last:
        pack_messages(parity_ref, *outs)


def message_shapes(size_x, size_y, own, depth):
    rows = SENT * max(size_x, size_y) * own
    return [jax.ShapeDtypeStruct((rows, depth), jnp.bfloat16)] * 4


def params():
    return pltpu.CompilerParams(vmem_limit_bytes=VMEM_BYTES)


def in_vmem(count):
    return [pl.BlockSpec(memory_space=pltpu.VMEM)] * count


def start(parity, orbital_block):
    own, size_x, size_y, depth = orbital_block.shape
    field = jax.ShapeDtypeStruct((size_x, size_y, own, depth), jnp.float32)
    return pl.pallas_call(
        start_kernel,
        out_shape=[field] + message_shapes(size_x, size_y, own, depth),
        in_specs=[pl.BlockSpec(memory_space=pltpu.SMEM)] + in_vmem(1),
        out_specs=in_vmem(5),
        compiler_params=params(),
    )(parity, orbital_block.reshape(own * size_x * size_y, depth))


def fixed_arrays(potential):
    depth = potential.shape[1]
    return pl.pallas_call(
        fixed_kernel,
        out_shape=[
            jax.ShapeDtypeStruct(potential.shape, jnp.float32),
            jax.ShapeDtypeStruct((2 * depth, depth), jnp.bfloat16),
            jax.ShapeDtypeStruct((depth, depth), jnp.bfloat16),
        ],
        in_specs=in_vmem(1),
        out_specs=in_vmem(3),
        compiler_params=params(),
        cost_estimate=pl.CostEstimate(
            flops=30 * depth * depth, bytes_accessed=16 * depth * depth, transcendentals=0
        ),
    )(potential)


def filter_step(parity, field, fixed, messages, previous, last):
    size_x, size_y, own, depth = field.shape
    field_shape = jax.ShapeDtypeStruct(field.shape, jnp.float32)
    before = [] if previous is None else [previous]
    inner = pl.pallas_call(
        functools.partial(inner_kernel, previous is not None),
        out_shape=field_shape,
        in_specs=in_vmem(4 + len(before)),
        out_specs=in_vmem(1)[0],
        compiler_params=params(),
        cost_estimate=pl.CostEstimate(
            flops=6 * field.size * depth, bytes_accessed=12 * field.size, transcendentals=0
        ),
    )(field, *fixed, *before)
    if last:
        out_shape = [jax.ShapeDtypeStruct((own, size_x * size_y * depth), jnp.float32)]
    else:
        out_shape = [field_shape] + message_shapes(size_x, size_y, own, depth)
    return pl.pallas_call(
        functools.partial(outer_kernel, 1.0 if previous is None else 2.0, last),
        out_shape=out_shape,
        in_specs=[pl.BlockSpec(memory_space=pltpu.SMEM)] + in_vmem(5),
        out_specs=in_vmem(len(out_shape)),
        scratch_shapes=[
            pltpu.VMEM((2 * WIDTH, size_y, own, depth), jnp.float32),
            pltpu.VMEM((size_x, 2 * WIDTH, own, depth), jnp.float32),
            pltpu.VMEM(field.shape, jnp.float32),
        ],
        compiler_params=params(),
    )(parity, inner, *messages)


def swap(y_odd, x_even, x_odd, y_even):
    def swapped(values, axis, first):
        count = lax.axis_size(axis)
        step = lambda i: 1 if (i - first) % 2 == 0 else -1
        return lax.ppermute(values, axis, [(i, (i + step(i)) % count) for i in range(count)])

    return (
        swapped(y_odd, "dy", 1),
        swapped(x_even, "dx", 0),
        swapped(x_odd, "dx", 1),
        swapped(y_even, "dy", 0),
    )


def sum_over_grid(values, sent_type):
    for axis in ("dx", "dy"):
        count = lax.axis_size(axis)
        sent = jnp.broadcast_to(values.astype(sent_type)[None], (count,) + values.shape)
        values = jnp.sum(lax.all_to_all(sent, axis, 0, 0).astype(jnp.float32), axis=0)
    return values


def sum_at_once(values):
    count = lax.axis_size("dx") * lax.axis_size("dy")
    flat = values.reshape(1, 1, values.size)
    sent = jnp.broadcast_to(flat, (count, 1, values.size))
    got = lax.all_to_all(sent, ("dx", "dy"), 0, 0, tiled=True)
    return jnp.sum(got, axis=0).reshape(values.shape)


def other_band(values):
    return lax.ppermute(values, "band", [(0, 1), (1, 0)])


def rows_dot(first, second, **kwargs):
    return lax.dot_general(
        first, second, (((1,), (1,)), ((), ())), preferred_element_type=jnp.float32, **kwargs
    )


def shards(orbital_block, potential, resident):
    own_count, size_x, size_y, depth = orbital_block.shape
    cell_count = size_x * size_y * depth
    flat_potential = potential.reshape(size_x * size_y, depth)
    parity = jnp.stack([lax.axis_index("dx") % 2, lax.axis_index("dy") % 2]).astype(jnp.int32)

    field, *messages = start(parity, orbital_block)
    fixed = fixed_arrays(flat_potential)
    previous = None
    for degree_step in range(DEGREE):
        last = degree_step == DEGREE - 1
        following, *messages = filter_step(
            parity, field, fixed, swap(*messages), previous, last
        )
        previous, field = field, following
    filtered = field

    rounded = filtered.astype(jnp.bfloat16)
    rounded_other = other_band(rounded)
    own_resident = resident.reshape(-1, cell_count)
    local_own = rows_dot(rounded, own_resident)
    local_other = rows_dot(rounded_other, own_resident)
    local = jnp.concatenate([local_own, local_other], axis=0) * SENT_SCALE
    correlations = (sum_over_grid(local, jnp.float16) / SENT_SCALE).astype(jnp.bfloat16)
    correction = jnp.dot(correlations, own_resident, preferred_element_type=jnp.float32)
    mine, theirs = correction[:own_count], correction[own_count:]
    sent = jnp.concatenate([theirs, mine], axis=0).astype(jnp.bfloat16)
    got = other_band(sent).astype(jnp.float32)
    projected = filtered - mine - got[:own_count]
    projected_other = rounded_other.astype(jnp.float32) - theirs - got[own_count:]
    exact = functools.partial(rows_dot, precision=lax.Precision.HIGHEST)
    partial_gram = exact(projected, jnp.concatenate([projected, projected_other], axis=0))
    turned = jnp.roll(partial_gram, own_count, axis=1)
    partial_gram = jnp.where(lax.axis_index("band") == 0, partial_gram, turned)
    total_cells = cell_count * lax.axis_size("dx") * lax.axis_size("dy")
    gram_matrix = sum_at_once(partial_gram) / total_cells
    return (projected.reshape(orbital_block.shape), gram_matrix)


def solution(mesh):
    placed = (P("band", "dx", "dy", None), P("dx", "dy", None), P("band", "dx", "dy", None))
    return jax.shard_map(
        shards,
        mesh=mesh,
        in_specs=placed,
        out_specs=(P("band", "dx", "dy", None), P("band", None)),
        check_vma=False,
    )
```

```python
import functools

import jax
import jax.numpy as jnp
from jax import lax
from jax.experimental import pallas as pl
from jax.experimental.pallas import tpu as pltpu
from jax.sharding import PartitionSpec as P

DEGREE = 4


STENCIL_WEIGHTS = (
    -5369.0 / 1800.0,
    12.0 / 7.0,
    -15.0 / 56.0,
    10.0 / 189.0,
    -1.0 / 112.0,
    2.0 / 1925.0,
    -1.0 / 16632.0,
)
FILTER_CENTER = 23.0
FILTER_HALF = 21.0
WIDTH = 6
SENT = WIDTH + 1
SENT_SCALE = 1.0 / 64.0
VMEM_BYTES = 8 * 1024 * 1024


def pack_layer(out_ref, at, layer):
    rows = layer.shape[0] * layer.shape[1]
    out_ref[at * rows : (at + 1) * rows, :] = layer.reshape(rows, layer.shape[2]).astype(
        jnp.bfloat16
    )


def pack_messages(parity_ref, field_ref, y_odd, x_even, x_odd, y_even):
    def layer(dim, at):
        return field_ref[at] if dim == 0 else field_ref[:, at]

    for dim, even, odd in ((0, x_even, x_odd), (1, y_even, y_odd)):
        size = field_ref.shape[dim]
        for out_ref, tail in ((even, 1 - parity_ref[dim]), (odd, parity_ref[dim])):
            for at in range(WIDTH):
                pack_layer(out_ref, at, layer(dim, tail * (size - WIDTH) + at))
            nearest = layer(dim, tail * (size - 1))
            used = SENT * nearest.shape[0] * nearest.shape[1]
            if used > out_ref.shape[0]:
                continue
            pack_layer(out_ref, WIDTH, nearest - nearest.astype(jnp.bfloat16).astype(jnp.float32))
            if used < out_ref.shape[0]:
                rows = out_ref.shape[0] - used
                out_ref[used:, :] = jnp.zeros((rows, out_ref.shape[1]), jnp.bfloat16)


def unpack_messages(parity_ref, halo_x, halo_y, y_odd, x_even, x_odd, y_even):
    for dim, halo, even, odd in ((0, halo_x, x_even, x_odd), (1, halo_y, y_even, y_odd)):
        shape = halo.shape[1:] if dim == 0 else halo.shape[:1] + halo.shape[2:]
        rows = shape[0] * shape[1]
        parity = parity_ref[dim]
        for got, after, near in ((even, 1 - parity, WIDTH - parity), (odd, parity, WIDTH - 1 + parity)):
            def read(at):
                return got[at * rows : (at + 1) * rows, :].astype(jnp.float32).reshape(shape)

            for at in range(WIDTH):
                place = after * WIDTH + at
                if dim == 0:
                    halo[place] = read(at)
                else:
                    halo[:, place] = read(at)
            if got.shape[0] < SENT * rows:
                continue
            if dim == 0:
                halo[near] += read(WIDTH)
            else:
                halo[:, near] += read(WIDTH)


def start_kernel(parity_ref, cells_ref, field_ref, *messages):
    size_x, size_y, own = field_ref.shape[:3]
    for x in range(size_x):
        for y in range(size_y):
            rows = pl.ds(x * size_y + y, own, stride=size_x * size_y)
            field_ref[x, y] = cells_ref[rows, :]
    pack_messages(parity_ref, field_ref, *messages)


def fixed_kernel(potential_ref, kept_ref, band_ref, rest_ref):
    depth = rest_ref.shape[0]
    kept_ref[...] = potential_ref[...]
    row = lax.broadcasted_iota(jnp.int32, (depth, depth), 0)
    away = jnp.abs(row - lax.broadcasted_iota(jnp.int32, (depth, depth), 1))
    weights = [-2.0 * w / FILTER_HALF for w in STENCIL_WEIGHTS]
    matrix = jnp.where(away == 0, 3.0 * weights[0] - FILTER_CENTER / FILTER_HALF, 0.0)
    for k in range(1, WIDTH + 1):
        matrix = jnp.where(away == k, weights[k], matrix)
    high = matrix.astype(jnp.bfloat16)
    band_ref[:depth, :] = high
    band_ref[depth:, :] = high
    rest_ref[...] = (matrix - high.astype(jnp.float32)).astype(jnp.bfloat16)


def inner_kernel(has_previous, field_ref, potential_ref, band_ref, rest_ref, *refs):
    previous_ref = refs[0] if has_previous else None
    total_ref = refs[-1]
    factor = 2.0 if has_previous else 1.0
    scale = factor / FILTER_HALF
    size_x, size_y, own, depth = field_ref.shape

    cells = field_ref[...].reshape(size_x * size_y * own, depth)
    high = cells.astype(jnp.bfloat16)
    low = (cells - high.astype(jnp.float32)).astype(jnp.bfloat16)
    along_z = jnp.dot(
        jnp.concatenate([high, low], axis=1), band_ref[...], preferred_element_type=jnp.float32
    ) + jnp.dot(high, rest_ref[...], preferred_element_type=jnp.float32)
    total_ref[...] = (factor * along_z).reshape(field_ref.shape)
    weights = [-2.0 * scale * w for w in STENCIL_WEIGHTS]

    def inside(total, line, at):
        for k in range(1, WIDTH + 1):
            near = [line[i] for i in (at - k, at + k) if 0 <= i < len(line)]
            if near:
                total = total + weights[k] * sum(near[1:], near[0])
        return total

    @pl.loop(0, size_y)
    def _(y):
        line = [field_ref[x, y] for x in range(size_x)]
        for x in range(size_x):
            total = total_ref[x, y]
            total = total + (scale * potential_ref[pl.ds(x * size_y + y, 1), :]) * line[x]
            if has_previous:
                total = total - previous_ref[x, y]
            total_ref[x, y] = inside(total, line, x)

    @pl.loop(0, size_x)
    def _(x):
        line = [field_ref[x, y] for y in range(size_y)]
        for y in range(size_y):
            total_ref[x, y] = inside(total_ref[x, y], line, y)


def outer_kernel(factor, last, parity_ref, inner_ref, *refs):
    messages, outs, (halo_x, halo_y, total_ref) = refs[:4], refs[4:-3], refs[-3:]
    size_x, size_y, own, depth = inner_ref.shape
    unpack_messages(parity_ref, halo_x, halo_y, *messages)
    weights = [-2.0 * factor / FILTER_HALF * w for w in STENCIL_WEIGHTS]

    def outside(total, line, at, size):
        for k in range(1, WIDTH + 1):
            if at - k < 0:
                total = total + weights[k] * line[WIDTH + at - k]
            if at + k >= size:
                total = total + weights[k] * line[WIDTH + at + k - size]
        return total

    @pl.loop(0, size_y)
    def _(y):
        line = [halo_x[k, y] for k in range(2 * WIDTH)]
        for x in range(size_x):
            total_ref[x, y] = outside(inner_ref[x, y], line, x, size_x)

    @pl.loop(0, size_x)
    def _(x):
        line = [halo_y[x, k] for k in range(2 * WIDTH)]
        for y in range(size_y):
            total = outside(total_ref[x, y], line, y, size_y)
            if last:
                place = pl.multiple_of((x * size_y + y) * depth, depth)
                outs[0][:, pl.ds(place, depth)] = total
            else:
                outs[0][x, y] = total

    if not last:
        pack_messages(parity_ref, *outs)


def message_shapes(size_x, size_y, own, depth):
    short = max(WIDTH * size_x, SENT * size_y) * own
    sizes = (SENT * size_x * own, short, short, WIDTH * size_x * own)
    return [jax.ShapeDtypeStruct((rows, depth), jnp.bfloat16) for rows in sizes]


def params():
    return pltpu.CompilerParams(vmem_limit_bytes=VMEM_BYTES)


def in_vmem(count):
    return [pl.BlockSpec(memory_space=pltpu.VMEM)] * count


def start(parity, orbital_block):
    own, size_x, size_y, depth = orbital_block.shape
    field = jax.ShapeDtypeStruct((size_x, size_y, own, depth), jnp.float32)
    return pl.pallas_call(
        start_kernel,
        out_shape=[field] + message_shapes(size_x, size_y, own, depth),
        in_specs=[pl.BlockSpec(memory_space=pltpu.SMEM)] + in_vmem(1),
        out_specs=in_vmem(5),
        compiler_params=params(),
    )(parity, orbital_block.reshape(own * size_x * size_y, depth))


def fixed_arrays(potential):
    depth = potential.shape[1]
    return pl.pallas_call(
        fixed_kernel,
        out_shape=[
            jax.ShapeDtypeStruct(potential.shape, jnp.float32),
            jax.ShapeDtypeStruct((2 * depth, depth), jnp.bfloat16),
            jax.ShapeDtypeStruct((depth, depth), jnp.bfloat16),
        ],
        in_specs=in_vmem(1),
        out_specs=in_vmem(3),
        compiler_params=params(),
        cost_estimate=pl.CostEstimate(
            flops=30 * depth * depth, bytes_accessed=16 * depth * depth, transcendentals=0
        ),
    )(potential)


def filter_step(parity, field, fixed, messages, previous, last):
    size_x, size_y, own, depth = field.shape
    field_shape = jax.ShapeDtypeStruct(field.shape, jnp.float32)
    before = [] if previous is None else [previous]
    inner = pl.pallas_call(
        functools.partial(inner_kernel, previous is not None),
        out_shape=field_shape,
        in_specs=in_vmem(4 + len(before)),
        out_specs=in_vmem(1)[0],
        compiler_params=params(),
        cost_estimate=pl.CostEstimate(
            flops=6 * field.size * depth, bytes_accessed=12 * field.size, transcendentals=0
        ),
    )(field, *fixed, *before)
    if last:
        out_shape = [jax.ShapeDtypeStruct((own, size_x * size_y * depth), jnp.float32)]
    else:
        out_shape = [field_shape] + message_shapes(size_x, size_y, own, depth)
    return pl.pallas_call(
        functools.partial(outer_kernel, 1.0 if previous is None else 2.0, last),
        out_shape=out_shape,
        in_specs=[pl.BlockSpec(memory_space=pltpu.SMEM)] + in_vmem(5),
        out_specs=in_vmem(len(out_shape)),
        scratch_shapes=[
            pltpu.VMEM((2 * WIDTH, size_y, own, depth), jnp.float32),
            pltpu.VMEM((size_x, 2 * WIDTH, own, depth), jnp.float32),
            pltpu.VMEM(field.shape, jnp.float32),
        ],
        compiler_params=params(),
    )(parity, inner, *messages)


def swap(y_odd, x_even, x_odd, y_even):
    def swapped(values, axis, first):
        count = lax.axis_size(axis)
        step = lambda i: 1 if (i - first) % 2 == 0 else -1
        return lax.ppermute(values, axis, [(i, (i + step(i)) % count) for i in range(count)])

    return (
        swapped(y_odd, "dy", 1),
        swapped(x_even, "dx", 0),
        swapped(x_odd, "dx", 1),
        swapped(y_even, "dy", 0),
    )


def sum_over_grid(values, sent_type):
    for axis in ("dx", "dy"):
        count = lax.axis_size(axis)
        sent = jnp.broadcast_to(values.astype(sent_type)[None], (count,) + values.shape)
        values = jnp.sum(lax.all_to_all(sent, axis, 0, 0).astype(jnp.float32), axis=0)
    return values


def other_band(values):
    return lax.ppermute(values, "band", [(0, 1), (1, 0)])


def rows_dot(first, second, **kwargs):
    return lax.dot_general(
        first, second, (((1,), (1,)), ((), ())), preferred_element_type=jnp.float32, **kwargs
    )


def shards(orbital_block, potential, resident):
    own_count, size_x, size_y, depth = orbital_block.shape
    cell_count = size_x * size_y * depth
    flat_potential = potential.reshape(size_x * size_y, depth)
    parity = jnp.stack([lax.axis_index("dx") % 2, lax.axis_index("dy") % 2]).astype(jnp.int32)

    field, *messages = start(parity, orbital_block)
    fixed = fixed_arrays(flat_potential)
    previous = None
    for degree_step in range(DEGREE):
        last = degree_step == DEGREE - 1
        following, *messages = filter_step(
            parity, field, fixed, swap(*messages), previous, last
        )
        previous, field = field, following
    filtered = field

    rounded = filtered.astype(jnp.bfloat16)
    rounded_other = other_band(rounded)
    own_resident = resident.reshape(-1, cell_count)
    local_own = rows_dot(rounded, own_resident)
    local_other = rows_dot(rounded_other, own_resident)
    local = jnp.concatenate([local_own, local_other], axis=0) * SENT_SCALE
    correlations = (sum_over_grid(local, jnp.float16) / SENT_SCALE).astype(jnp.bfloat16)
    correction = jnp.dot(correlations, own_resident, preferred_element_type=jnp.float32)
    mine, theirs = correction[:own_count], correction[own_count:]
    got = other_band(theirs.astype(jnp.bfloat16)).astype(jnp.float32)
    got_other = other_band(mine.astype(jnp.bfloat16)).astype(jnp.float32)
    projected = filtered - mine - got
    projected_other = rounded_other.astype(jnp.float32) - theirs - got_other
    exact = functools.partial(rows_dot, precision=lax.Precision.HIGHEST)
    partial_gram = exact(projected, jnp.concatenate([projected, projected_other], axis=0))
    turned = jnp.roll(partial_gram, own_count, axis=1)
    partial_gram = jnp.where(lax.axis_index("band") == 0, partial_gram, turned)
    lanes = 128
    partial_gram = jnp.pad(partial_gram, ((0, 0), (0, lanes - 2 * own_count)))
    total_cells = cell_count * lax.axis_size("dx") * lax.axis_size("dy")
    gram_matrix = sum_over_grid(partial_gram, jnp.float32)[:, : 2 * own_count] / total_cells
    return (projected.reshape(orbital_block.shape), gram_matrix)


def solution(mesh):
    placed = (P("band", "dx", "dy", None), P("dx", "dy", None), P("band", "dx", "dy", None))
    return jax.shard_map(
        shards,
        mesh=mesh,
        in_specs=placed,
        out_specs=(P("band", "dx", "dy", None), P("band", None)),
        check_vma=False,
    )
```

```python
import functools

import jax
import jax.numpy as jnp
from jax import lax
from jax.experimental import pallas as pl
from jax.experimental.pallas import tpu as pltpu
from jax.sharding import PartitionSpec as P

DEGREE = 4


STENCIL_WEIGHTS = (
    -5369.0 / 1800.0,
    12.0 / 7.0,
    -15.0 / 56.0,
    10.0 / 189.0,
    -1.0 / 112.0,
    2.0 / 1925.0,
    -1.0 / 16632.0,
)
FILTER_CENTER = 23.0
FILTER_HALF = 21.0
WIDTH = 6
SENT = WIDTH + 1
SENT_SCALE = 1.0 / 64.0
VMEM_BYTES = 8 * 1024 * 1024


def pack_layer(out_ref, at, layer):
    rows = layer.shape[0] * layer.shape[1]
    out_ref[at * rows : (at + 1) * rows, :] = layer.reshape(rows, layer.shape[2]).astype(
        jnp.bfloat16
    )


def pack_messages(parity_ref, field_ref, x_even, y_odd, x_odd, y_even):
    def layer(dim, at):
        return field_ref[at] if dim == 0 else field_ref[:, at]

    for dim, even, odd in ((0, x_even, x_odd), (1, y_even, y_odd)):
        size = field_ref.shape[dim]
        for out_ref, tail in ((even, 1 - parity_ref[dim]), (odd, parity_ref[dim])):
            for at in range(WIDTH):
                pack_layer(out_ref, at, layer(dim, tail * (size - WIDTH) + at))
            nearest = layer(dim, tail * (size - 1))
            used = SENT * nearest.shape[0] * nearest.shape[1]
            if used > out_ref.shape[0]:
                continue
            pack_layer(out_ref, WIDTH, nearest - nearest.astype(jnp.bfloat16).astype(jnp.float32))
            if used < out_ref.shape[0]:
                rows = out_ref.shape[0] - used
                out_ref[used:, :] = jnp.zeros((rows, out_ref.shape[1]), jnp.bfloat16)


def unpack_messages(parity_ref, halo_x, halo_y, x_even, y_odd, x_odd, y_even):
    for dim, halo, even, odd in ((0, halo_x, x_even, x_odd), (1, halo_y, y_even, y_odd)):
        shape = halo.shape[1:] if dim == 0 else halo.shape[:1] + halo.shape[2:]
        rows = shape[0] * shape[1]
        parity = parity_ref[dim]
        for got, after, near in ((even, 1 - parity, WIDTH - parity), (odd, parity, WIDTH - 1 + parity)):
            def read(at):
                return got[at * rows : (at + 1) * rows, :].astype(jnp.float32).reshape(shape)

            for at in range(WIDTH):
                place = after * WIDTH + at
                if dim == 0:
                    halo[place] = read(at)
                else:
                    halo[:, place] = read(at)
            if got.shape[0] < SENT * rows:
                continue
            if dim == 0:
                halo[near] += read(WIDTH)
            else:
                halo[:, near] += read(WIDTH)


def start_kernel(parity_ref, cells_ref, field_ref, *messages):
    size_x, size_y, own = field_ref.shape[:3]
    for x in range(size_x):
        for y in range(size_y):
            rows = pl.ds(x * size_y + y, own, stride=size_x * size_y)
            field_ref[x, y] = cells_ref[rows, :]
    pack_messages(parity_ref, field_ref, *messages)


def fixed_kernel(potential_ref, kept_ref, band_ref, rest_ref):
    depth = rest_ref.shape[0]
    kept_ref[...] = potential_ref[...]
    row = lax.broadcasted_iota(jnp.int32, (depth, depth), 0)
    away = jnp.abs(row - lax.broadcasted_iota(jnp.int32, (depth, depth), 1))
    weights = [-2.0 * w / FILTER_HALF for w in STENCIL_WEIGHTS]
    matrix = jnp.where(away == 0, 3.0 * weights[0] - FILTER_CENTER / FILTER_HALF, 0.0)
    for k in range(1, WIDTH + 1):
        matrix = jnp.where(away == k, weights[k], matrix)
    high = matrix.astype(jnp.bfloat16)
    band_ref[:depth, :] = high
    band_ref[depth:, :] = high
    rest_ref[...] = (matrix - high.astype(jnp.float32)).astype(jnp.bfloat16)


def inner_kernel(has_previous, field_ref, potential_ref, band_ref, rest_ref, *refs):
    previous_ref = refs[0] if has_previous else None
    total_ref = refs[-1]
    factor = 2.0 if has_previous else 1.0
    scale = factor / FILTER_HALF
    size_x, size_y, own, depth = field_ref.shape

    cells = field_ref[...].reshape(size_x * size_y * own, depth)
    high = cells.astype(jnp.bfloat16)
    low = (cells - high.astype(jnp.float32)).astype(jnp.bfloat16)
    along_z = jnp.dot(
        jnp.concatenate([high, low], axis=1), band_ref[...], preferred_element_type=jnp.float32
    ) + jnp.dot(high, rest_ref[...], preferred_element_type=jnp.float32)
    total_ref[...] = (factor * along_z).reshape(field_ref.shape)
    weights = [-2.0 * scale * w for w in STENCIL_WEIGHTS]

    def inside(total, line, at):
        for k in range(1, WIDTH + 1):
            near = [line[i] for i in (at - k, at + k) if 0 <= i < len(line)]
            if near:
                total = total + weights[k] * sum(near[1:], near[0])
        return total

    @pl.loop(0, size_y)
    def _(y):
        line = [field_ref[x, y] for x in range(size_x)]
        for x in range(size_x):
            total = total_ref[x, y]
            total = total + (scale * potential_ref[pl.ds(x * size_y + y, 1), :]) * line[x]
            if has_previous:
                total = total - previous_ref[x, y]
            total_ref[x, y] = inside(total, line, x)

    @pl.loop(0, size_x)
    def _(x):
        line = [field_ref[x, y] for y in range(size_y)]
        for y in range(size_y):
            total_ref[x, y] = inside(total_ref[x, y], line, y)


def outer_kernel(factor, last, parity_ref, inner_ref, *refs):
    messages, outs, (halo_x, halo_y, total_ref) = refs[:4], refs[4:-3], refs[-3:]
    size_x, size_y, own, depth = inner_ref.shape
    unpack_messages(parity_ref, halo_x, halo_y, *messages)
    weights = [-2.0 * factor / FILTER_HALF * w for w in STENCIL_WEIGHTS]

    def outside(total, line, at, size):
        for k in range(1, WIDTH + 1):
            if at - k < 0:
                total = total + weights[k] * line[WIDTH + at - k]
            if at + k >= size:
                total = total + weights[k] * line[WIDTH + at + k - size]
        return total

    @pl.loop(0, size_y)
    def _(y):
        line = [halo_x[k, y] for k in range(2 * WIDTH)]
        for x in range(size_x):
            total_ref[x, y] = outside(inner_ref[x, y], line, x, size_x)

    @pl.loop(0, size_x)
    def _(x):
        line = [halo_y[x, k] for k in range(2 * WIDTH)]
        for y in range(size_y):
            total = outside(total_ref[x, y], line, y, size_y)
            if last:
                place = pl.multiple_of((x * size_y + y) * depth, depth)
                outs[0][:, pl.ds(place, depth)] = total
            else:
                outs[0][x, y] = total

    if not last:
        pack_messages(parity_ref, *outs)


def message_shapes(size_x, size_y, own, depth):
    short = max(WIDTH * size_x, SENT * size_y) * own
    long = max(SENT * size_x, SENT * size_y) * own
    sizes = (long, SENT * size_x * own, short, WIDTH * size_x * own)
    return [jax.ShapeDtypeStruct((rows, depth), jnp.bfloat16) for rows in sizes]


def params():
    return pltpu.CompilerParams(vmem_limit_bytes=VMEM_BYTES)


def in_vmem(count):
    return [pl.BlockSpec(memory_space=pltpu.VMEM)] * count


def start(parity, orbital_block):
    own, size_x, size_y, depth = orbital_block.shape
    field = jax.ShapeDtypeStruct((size_x, size_y, own, depth), jnp.float32)
    return pl.pallas_call(
        start_kernel,
        out_shape=[field] + message_shapes(size_x, size_y, own, depth),
        in_specs=[pl.BlockSpec(memory_space=pltpu.SMEM)] + in_vmem(1),
        out_specs=in_vmem(5),
        compiler_params=params(),
    )(parity, orbital_block.reshape(own * size_x * size_y, depth))


def fixed_arrays(potential):
    depth = potential.shape[1]
    return pl.pallas_call(
        fixed_kernel,
        out_shape=[
            jax.ShapeDtypeStruct(potential.shape, jnp.float32),
            jax.ShapeDtypeStruct((2 * depth, depth), jnp.bfloat16),
            jax.ShapeDtypeStruct((depth, depth), jnp.bfloat16),
        ],
        in_specs=in_vmem(1),
        out_specs=in_vmem(3),
        compiler_params=params(),
        cost_estimate=pl.CostEstimate(
            flops=30 * depth * depth, bytes_accessed=16 * depth * depth, transcendentals=0
        ),
    )(potential)


def filter_step(parity, field, fixed, messages, previous, last):
    size_x, size_y, own, depth = field.shape
    field_shape = jax.ShapeDtypeStruct(field.shape, jnp.float32)
    before = [] if previous is None else [previous]
    inner = pl.pallas_call(
        functools.partial(inner_kernel, previous is not None),
        out_shape=field_shape,
        in_specs=in_vmem(4 + len(before)),
        out_specs=in_vmem(1)[0],
        compiler_params=params(),
        cost_estimate=pl.CostEstimate(
            flops=6 * field.size * depth, bytes_accessed=12 * field.size, transcendentals=0
        ),
    )(field, *fixed, *before)
    if last:
        out_shape = [jax.ShapeDtypeStruct((own, size_x * size_y * depth), jnp.float32)]
    else:
        out_shape = [field_shape] + message_shapes(size_x, size_y, own, depth)
    return pl.pallas_call(
        functools.partial(outer_kernel, 1.0 if previous is None else 2.0, last),
        out_shape=out_shape,
        in_specs=[pl.BlockSpec(memory_space=pltpu.SMEM)] + in_vmem(5),
        out_specs=in_vmem(len(out_shape)),
        scratch_shapes=[
            pltpu.VMEM((2 * WIDTH, size_y, own, depth), jnp.float32),
            pltpu.VMEM((size_x, 2 * WIDTH, own, depth), jnp.float32),
            pltpu.VMEM(field.shape, jnp.float32),
        ],
        compiler_params=params(),
    )(parity, inner, *messages)


def swap(x_even, y_odd, x_odd, y_even):
    def swapped(values, axis, first):
        count = lax.axis_size(axis)
        step = lambda i: 1 if (i - first) % 2 == 0 else -1
        return lax.ppermute(values, axis, [(i, (i + step(i)) % count) for i in range(count)])

    return (
        swapped(x_even, "dx", 0),
        swapped(y_odd, "dy", 1),
        swapped(x_odd, "dx", 1),
        swapped(y_even, "dy", 0),
    )


def sum_over_grid(values, sent_type):
    for axis in ("dx", "dy"):
        count = lax.axis_size(axis)
        sent = jnp.broadcast_to(values.astype(sent_type)[None], (count,) + values.shape)
        values = jnp.sum(lax.all_to_all(sent, axis, 0, 0).astype(jnp.float32), axis=0)
    return values


def other_band(values):
    return lax.ppermute(values, "band", [(0, 1), (1, 0)])


def rows_dot(first, second, **kwargs):
    return lax.dot_general(
        first, second, (((1,), (1,)), ((), ())), preferred_element_type=jnp.float32, **kwargs
    )


def shards(orbital_block, potential, resident):
    own_count, size_x, size_y, depth = orbital_block.shape
    cell_count = size_x * size_y * depth
    flat_potential = potential.reshape(size_x * size_y, depth)
    parity = jnp.stack([lax.axis_index("dx") % 2, lax.axis_index("dy") % 2]).astype(jnp.int32)

    field, *messages = start(parity, orbital_block)
    fixed = fixed_arrays(flat_potential)
    previous = None
    for degree_step in range(DEGREE):
        last = degree_step == DEGREE - 1
        following, *messages = filter_step(
            parity, field, fixed, swap(*messages), previous, last
        )
        previous, field = field, following
    filtered = field

    rounded = filtered.astype(jnp.bfloat16)
    rounded_other = other_band(rounded)
    own_resident = resident.reshape(-1, cell_count)
    local_own = rows_dot(rounded, own_resident)
    local_other = rows_dot(rounded_other, own_resident)
    local = jnp.concatenate([local_own, local_other], axis=0) * SENT_SCALE
    correlations = (sum_over_grid(local, jnp.float16) / SENT_SCALE).astype(jnp.bfloat16)
    correction = jnp.dot(correlations, own_resident, preferred_element_type=jnp.float32)
    mine, theirs = correction[:own_count], correction[own_count:]
    got = other_band(theirs.astype(jnp.bfloat16)).astype(jnp.float32)
    got_other = other_band(mine.astype(jnp.bfloat16)).astype(jnp.float32)
    projected = filtered - mine - got
    projected_other = rounded_other.astype(jnp.float32) - theirs - got_other
    exact = functools.partial(rows_dot, precision=lax.Precision.HIGH)
    partial_gram = exact(projected, jnp.concatenate([projected, projected_other], axis=0))
    turned = jnp.roll(partial_gram, own_count, axis=1)
    partial_gram = jnp.where(lax.axis_index("band") == 0, partial_gram, turned)
    lanes = 128
    partial_gram = jnp.pad(partial_gram, ((0, 0), (0, lanes - 2 * own_count)))
    total_cells = cell_count * lax.axis_size("dx") * lax.axis_size("dy")
    gram_matrix = sum_over_grid(partial_gram, jnp.float32)[:, : 2 * own_count] / total_cells
    return (projected.reshape(orbital_block.shape), gram_matrix)


def solution(mesh):
    placed = (P("band", "dx", "dy", None), P("dx", "dy", None), P("band", "dx", "dy", None))
    return jax.shard_map(
        shards,
        mesh=mesh,
        in_specs=placed,
        out_specs=(P("band", "dx", "dy", None), P("band", None)),
        check_vma=False,
    )
```

```python
import functools

import jax
import jax.numpy as jnp
from jax import lax
from jax.experimental import pallas as pl
from jax.experimental.pallas import tpu as pltpu
from jax.sharding import PartitionSpec as P

DEGREE = 4


STENCIL_WEIGHTS = (
    -5369.0 / 1800.0,
    12.0 / 7.0,
    -15.0 / 56.0,
    10.0 / 189.0,
    -1.0 / 112.0,
    2.0 / 1925.0,
    -1.0 / 16632.0,
)
FILTER_CENTER = 23.0
FILTER_HALF = 21.0
WIDTH = 6
SENT = WIDTH + 1
SENT_SCALE = 1.0 / 64.0
VMEM_BYTES = 8 * 1024 * 1024


def pack_layer(out_ref, at, layer):
    rows = layer.shape[0] * layer.shape[1]
    out_ref[at * rows : (at + 1) * rows, :] = layer.reshape(rows, layer.shape[2]).astype(
        jnp.bfloat16
    )


def pack_messages(parity_ref, field_ref, y_odd, x_even, x_odd, y_even):
    def layer(dim, at):
        return field_ref[at] if dim == 0 else field_ref[:, at]

    for dim, even, odd in ((0, x_even, x_odd), (1, y_even, y_odd)):
        size = field_ref.shape[dim]
        for out_ref, tail in ((even, 1 - parity_ref[dim]), (odd, parity_ref[dim])):
            for at in range(WIDTH):
                pack_layer(out_ref, at, layer(dim, tail * (size - WIDTH) + at))
            nearest = layer(dim, tail * (size - 1))
            used = SENT * nearest.shape[0] * nearest.shape[1]
            if used > out_ref.shape[0]:
                continue
            pack_layer(out_ref, WIDTH, nearest - nearest.astype(jnp.bfloat16).astype(jnp.float32))
            if used < out_ref.shape[0]:
                rows = out_ref.shape[0] - used
                out_ref[used:, :] = jnp.zeros((rows, out_ref.shape[1]), jnp.bfloat16)


def unpack(got, halo, dim, base, near):
    shape = halo.shape[1:] if dim == 0 else halo.shape[:1] + halo.shape[2:]
    rows = shape[0] * shape[1]

    def read(at):
        return got[at * rows : (at + 1) * rows, :].astype(jnp.float32).reshape(shape)

    for at in range(WIDTH):
        if dim == 0:
            halo[base + at] = read(at)
        else:
            halo[:, base + at] = read(at)
    if got.shape[0] >= SENT * rows:
        if dim == 0:
            halo[near] += read(WIDTH)
        else:
            halo[:, near] += read(WIDTH)


def start_kernel(parity_ref, cells_ref, field_ref, *messages):
    size_x, size_y, own = field_ref.shape[:3]
    for x in range(size_x):
        for y in range(size_y):
            rows = pl.ds(x * size_y + y, own, stride=size_x * size_y)
            field_ref[x, y] = cells_ref[rows, :]
    pack_messages(parity_ref, field_ref, *messages)


def fixed_kernel(potential_ref, kept_ref, band_ref, rest_ref):
    depth = rest_ref.shape[0]
    kept_ref[...] = potential_ref[...]
    row = lax.broadcasted_iota(jnp.int32, (depth, depth), 0)
    away = jnp.abs(row - lax.broadcasted_iota(jnp.int32, (depth, depth), 1))
    weights = [-2.0 * w / FILTER_HALF for w in STENCIL_WEIGHTS]
    matrix = jnp.where(away == 0, 3.0 * weights[0] - FILTER_CENTER / FILTER_HALF, 0.0)
    for k in range(1, WIDTH + 1):
        matrix = jnp.where(away == k, weights[k], matrix)
    high = matrix.astype(jnp.bfloat16)
    band_ref[:depth, :] = high
    band_ref[depth:, :] = high
    rest_ref[...] = (matrix - high.astype(jnp.float32)).astype(jnp.bfloat16)


def inner_kernel(has_previous, field_ref, potential_ref, band_ref, rest_ref, *refs):
    previous_ref = refs[0] if has_previous else None
    total_ref = refs[-1]
    factor = 2.0 if has_previous else 1.0
    scale = factor / FILTER_HALF
    size_x, size_y, own, depth = field_ref.shape

    cells = field_ref[...].reshape(size_x * size_y * own, depth)
    high = cells.astype(jnp.bfloat16)
    low = (cells - high.astype(jnp.float32)).astype(jnp.bfloat16)
    along_z = jnp.dot(
        jnp.concatenate([high, low], axis=1), band_ref[...], preferred_element_type=jnp.float32
    ) + jnp.dot(high, rest_ref[...], preferred_element_type=jnp.float32)
    total_ref[...] = (factor * along_z).reshape(field_ref.shape)
    weights = [-2.0 * scale * w for w in STENCIL_WEIGHTS]

    def inside(total, line, at):
        for k in range(1, WIDTH + 1):
            near = [line[i] for i in (at - k, at + k) if 0 <= i < len(line)]
            if near:
                total = total + weights[k] * sum(near[1:], near[0])
        return total

    @pl.loop(0, size_y)
    def _(y):
        line = [field_ref[x, y] for x in range(size_x)]
        for x in range(size_x):
            total = total_ref[x, y]
            total = total + (scale * potential_ref[pl.ds(x * size_y + y, 1), :]) * line[x]
            if has_previous:
                total = total - previous_ref[x, y]
            total_ref[x, y] = inside(total, line, x)

    @pl.loop(0, size_x)
    def _(x):
        line = [field_ref[x, y] for y in range(size_y)]
        for y in range(size_y):
            total_ref[x, y] = inside(total_ref[x, y], line, y)


def add_side(right, halo, source, weights, store):
    size_x, size_y = source.shape[:2]

    @pl.loop(0, size_y)
    def _(y):
        line = [halo[k, y] for k in range(WIDTH)]
        for i in range(WIDTH):
            x = size_x - WIDTH + i if right else i
            total = source[x, y]
            for k in range(1, WIDTH + 1):
                if right and x + k >= size_x:
                    total = total + weights[k] * line[x + k - size_x]
                if not right and x - k < 0:
                    total = total + weights[k] * line[WIDTH + x - k]
            store(x, y, total)


def outer_first_kernel(factor, parity_ref, inner_ref, y_odd, x_even, y_even, total_ref, halo_x, halo_y):
    size_x, size_y, own, depth = inner_ref.shape
    weights = [-2.0 * factor / FILTER_HALF * w for w in STENCIL_WEIGHTS]
    odd = parity_ref[1]
    unpack(y_odd, halo_y, 1, odd * WIDTH, WIDTH - 1 + odd)
    unpack(y_even, halo_y, 1, (1 - odd) * WIDTH, WIDTH - odd)
    odd_x = parity_ref[0]
    unpack(x_even, halo_x, 0, 0, odd_x * (WIDTH - 1))

    @pl.loop(0, size_x)
    def _(x):
        line = [halo_y[x, k] for k in range(2 * WIDTH)]
        for y in range(size_y):
            total = inner_ref[x, y]
            for k in range(1, WIDTH + 1):
                if y - k < 0:
                    total = total + weights[k] * line[WIDTH + y - k]
                if y + k >= size_y:
                    total = total + weights[k] * line[WIDTH + y + k - size_y]
            total_ref[x, y] = total

    def store(x, y, total):
        total_ref[x, y] = total

    @pl.when(odd_x == 0)
    def _():
        add_side(True, halo_x, total_ref, weights, store)

    @pl.when(odd_x == 1)
    def _():
        add_side(False, halo_x, total_ref, weights, store)


def outer_last_kernel(factor, last, parity_ref, total_ref, x_odd, *refs):
    outs, halo_x = refs[:-1], refs[-1]
    size_x, size_y, own, depth = total_ref.shape
    weights = [-2.0 * factor / FILTER_HALF * w for w in STENCIL_WEIGHTS]
    odd_x = parity_ref[0]
    unpack(x_odd, halo_x, 0, 0, (1 - odd_x) * (WIDTH - 1))

    def store(x, y, total):
        if last:
            place = pl.multiple_of((x * size_y + y) * depth, depth)
            outs[0][:, pl.ds(place, depth)] = total
        else:
            outs[0][x, y] = total

    def keep(first):
        @pl.loop(0, size_y)
        def _(y):
            for x in range(first, first + size_x - WIDTH):
                store(x, y, total_ref[x, y])

    @pl.when(odd_x == 1)
    def _():
        add_side(True, halo_x, total_ref, weights, store)
        keep(0)

    @pl.when(odd_x == 0)
    def _():
        add_side(False, halo_x, total_ref, weights, store)
        keep(WIDTH)

    if not last:
        pack_messages(parity_ref, *outs)


def message_shapes(size_x, size_y, own, depth):
    short = max(WIDTH * size_x, SENT * size_y) * own
    long = SENT * size_x * own
    sizes = (long, max(long, short), (long + short) // 2 // 16 * 16, WIDTH * size_x * own)
    return [jax.ShapeDtypeStruct((rows, depth), jnp.bfloat16) for rows in sizes]


def params():
    return pltpu.CompilerParams(vmem_limit_bytes=VMEM_BYTES)


def in_vmem(count):
    return [pl.BlockSpec(memory_space=pltpu.VMEM)] * count


def start(parity, orbital_block):
    own, size_x, size_y, depth = orbital_block.shape
    field = jax.ShapeDtypeStruct((size_x, size_y, own, depth), jnp.float32)
    return pl.pallas_call(
        start_kernel,
        out_shape=[field] + message_shapes(size_x, size_y, own, depth),
        in_specs=[pl.BlockSpec(memory_space=pltpu.SMEM)] + in_vmem(1),
        out_specs=in_vmem(5),
        compiler_params=params(),
    )(parity, orbital_block.reshape(own * size_x * size_y, depth))


def fixed_arrays(potential):
    depth = potential.shape[1]
    return pl.pallas_call(
        fixed_kernel,
        out_shape=[
            jax.ShapeDtypeStruct(potential.shape, jnp.float32),
            jax.ShapeDtypeStruct((2 * depth, depth), jnp.bfloat16),
            jax.ShapeDtypeStruct((depth, depth), jnp.bfloat16),
        ],
        in_specs=in_vmem(1),
        out_specs=in_vmem(3),
        compiler_params=params(),
        cost_estimate=pl.CostEstimate(
            flops=30 * depth * depth, bytes_accessed=16 * depth * depth, transcendentals=0
        ),
    )(potential)


def filter_step(parity, field, fixed, messages, previous, last):
    size_x, size_y, own, depth = field.shape
    field_shape = jax.ShapeDtypeStruct(field.shape, jnp.float32)
    before = [] if previous is None else [previous]
    inner = pl.pallas_call(
        functools.partial(inner_kernel, previous is not None),
        out_shape=field_shape,
        in_specs=in_vmem(4 + len(before)),
        out_specs=in_vmem(1)[0],
        compiler_params=params(),
        cost_estimate=pl.CostEstimate(
            flops=6 * field.size * depth, bytes_accessed=12 * field.size, transcendentals=0
        ),
    )(field, *fixed, *before)
    y_odd, x_even, x_odd, y_even = messages
    factor = 1.0 if previous is None else 2.0
    scratch_x = pltpu.VMEM((WIDTH, size_y, own, depth), jnp.float32)
    scratch_y = pltpu.VMEM((size_x, 2 * WIDTH, own, depth), jnp.float32)
    smem = pl.BlockSpec(memory_space=pltpu.SMEM)
    total = pl.pallas_call(
        functools.partial(outer_first_kernel, factor),
        out_shape=field_shape,
        in_specs=[smem] + in_vmem(4),
        out_specs=in_vmem(1)[0],
        scratch_shapes=[scratch_x, scratch_y],
        compiler_params=params(),
        cost_estimate=pl.CostEstimate(
            flops=field.size, bytes_accessed=field.size, transcendentals=0
        ),
    )(parity, inner, y_odd, x_even, y_even)
    if last:
        out_shape = [jax.ShapeDtypeStruct((own, size_x * size_y * depth), jnp.float32)]
    else:
        out_shape = [field_shape] + message_shapes(size_x, size_y, own, depth)
    return pl.pallas_call(
        functools.partial(outer_last_kernel, factor, last),
        out_shape=out_shape,
        in_specs=[smem] + in_vmem(2),
        out_specs=in_vmem(len(out_shape)),
        scratch_shapes=[scratch_x],
        compiler_params=params(),
    )(parity, total, x_odd)


def swap(y_odd, x_even, x_odd, y_even):
    def swapped(values, axis, first):
        count = lax.axis_size(axis)
        step = lambda i: 1 if (i - first) % 2 == 0 else -1
        return lax.ppermute(values, axis, [(i, (i + step(i)) % count) for i in range(count)])

    return (
        swapped(y_odd, "dy", 1),
        swapped(x_even, "dx", 0),
        swapped(x_odd, "dx", 1),
        swapped(y_even, "dy", 0),
    )


def sum_over_grid(values, sent_type):
    for axis in ("dx", "dy"):
        count = lax.axis_size(axis)
        sent = jnp.broadcast_to(values.astype(sent_type)[None], (count,) + values.shape)
        values = jnp.sum(lax.all_to_all(sent, axis, 0, 0).astype(jnp.float32), axis=0)
    return values


def other_band(values):
    return lax.ppermute(values, "band", [(0, 1), (1, 0)])


def rows_dot(first, second, **kwargs):
    return lax.dot_general(
        first, second, (((1,), (1,)), ((), ())), preferred_element_type=jnp.float32, **kwargs
    )


def shards(orbital_block, potential, resident):
    own_count, size_x, size_y, depth = orbital_block.shape
    cell_count = size_x * size_y * depth
    flat_potential = potential.reshape(size_x * size_y, depth)
    parity = jnp.stack([lax.axis_index("dx") % 2, lax.axis_index("dy") % 2]).astype(jnp.int32)

    field, *messages = start(parity, orbital_block)
    fixed = fixed_arrays(flat_potential)
    previous = None
    for degree_step in range(DEGREE):
        last = degree_step == DEGREE - 1
        following, *messages = filter_step(
            parity, field, fixed, swap(*messages), previous, last
        )
        previous, field = field, following
    filtered = field

    rounded = filtered.astype(jnp.bfloat16)
    rounded_other = other_band(rounded)
    own_resident = resident.reshape(-1, cell_count)
    local_own = rows_dot(rounded, own_resident)
    local_other = rows_dot(rounded_other, own_resident)
    local = jnp.concatenate([local_own, local_other], axis=0) * SENT_SCALE
    correlations = (sum_over_grid(local, jnp.float16) / SENT_SCALE).astype(jnp.bfloat16)
    correction = jnp.dot(correlations, own_resident, preferred_element_type=jnp.float32)
    mine, theirs = correction[:own_count], correction[own_count:]
    got = other_band(theirs.astype(jnp.bfloat16)).astype(jnp.float32)
    got_other = other_band(mine.astype(jnp.bfloat16)).astype(jnp.float32)
    projected = filtered - mine - got
    projected_other = rounded_other.astype(jnp.float32) - theirs - got_other
    exact = functools.partial(rows_dot, precision=lax.Precision.HIGH)
    partial_gram = exact(projected, jnp.concatenate([projected, projected_other], axis=0))
    turned = jnp.roll(partial_gram, own_count, axis=1)
    partial_gram = jnp.where(lax.axis_index("band") == 0, partial_gram, turned)
    lanes = 128
    partial_gram = jnp.pad(partial_gram, ((0, 0), (0, lanes - 2 * own_count)))
    total_cells = cell_count * lax.axis_size("dx") * lax.axis_size("dy")
    gram_matrix = sum_over_grid(partial_gram, jnp.float32)[:, : 2 * own_count] / total_cells
    return (projected.reshape(orbital_block.shape), gram_matrix)


def solution(mesh):
    placed = (P("band", "dx", "dy", None), P("dx", "dy", None), P("band", "dx", "dy", None))
    return jax.shard_map(
        shards,
        mesh=mesh,
        in_specs=placed,
        out_specs=(P("band", "dx", "dy", None), P("band", None)),
        check_vma=False,
    )
```

```python
import functools

import jax
import jax.numpy as jnp
from jax import lax
from jax.experimental import pallas as pl
from jax.experimental.pallas import tpu as pltpu
from jax.sharding import PartitionSpec as P

DEGREE = 4


STENCIL_WEIGHTS = (
    -5369.0 / 1800.0,
    12.0 / 7.0,
    -15.0 / 56.0,
    10.0 / 189.0,
    -1.0 / 112.0,
    2.0 / 1925.0,
    -1.0 / 16632.0,
)
FILTER_CENTER = 23.0
FILTER_HALF = 21.0
WIDTH = 6
SENT = WIDTH + 1
SENT_SCALE = 1.0 / 64.0
VMEM_BYTES = 8 * 1024 * 1024


def pack_layer(out_ref, at, layer):
    rows = layer.shape[0] * layer.shape[1]
    out_ref[at * rows : (at + 1) * rows, :] = layer.reshape(rows, layer.shape[2]).astype(
        jnp.bfloat16
    )


def pack_messages(parity_ref, field_ref, y_odd, x_even, x_odd, y_even):
    def layer(dim, at):
        return field_ref[at] if dim == 0 else field_ref[:, at]

    for dim, even, odd in ((0, x_even, x_odd), (1, y_even, y_odd)):
        size = field_ref.shape[dim]
        for out_ref, tail in ((even, 1 - parity_ref[dim]), (odd, parity_ref[dim])):
            for at in range(WIDTH):
                pack_layer(out_ref, at, layer(dim, tail * (size - WIDTH) + at))
            nearest = layer(dim, tail * (size - 1))
            used = SENT * nearest.shape[0] * nearest.shape[1]
            if used > out_ref.shape[0]:
                continue
            pack_layer(out_ref, WIDTH, nearest - nearest.astype(jnp.bfloat16).astype(jnp.float32))
            if used < out_ref.shape[0]:
                rows = out_ref.shape[0] - used
                out_ref[used:, :] = jnp.zeros((rows, out_ref.shape[1]), jnp.bfloat16)


def unpack(got, halo, dim, base, near):
    shape = halo.shape[1:] if dim == 0 else halo.shape[:1] + halo.shape[2:]
    rows = shape[0] * shape[1]

    def read(at):
        return got[at * rows : (at + 1) * rows, :].astype(jnp.float32).reshape(shape)

    for at in range(WIDTH):
        if dim == 0:
            halo[base + at] = read(at)
        else:
            halo[:, base + at] = read(at)
    if got.shape[0] >= SENT * rows:
        if dim == 0:
            halo[near] += read(WIDTH)
        else:
            halo[:, near] += read(WIDTH)


def start_kernel(parity_ref, cells_ref, field_ref, *messages):
    size_x, size_y, own = field_ref.shape[:3]
    for x in range(size_x):
        for y in range(size_y):
            rows = pl.ds(x * size_y + y, own, stride=size_x * size_y)
            field_ref[x, y] = cells_ref[rows, :]
    pack_messages(parity_ref, field_ref, *messages)


def fixed_kernel(potential_ref, kept_ref, band_ref, rest_ref):
    depth = rest_ref.shape[0]
    kept_ref[...] = potential_ref[...]
    row = lax.broadcasted_iota(jnp.int32, (depth, depth), 0)
    away = jnp.abs(row - lax.broadcasted_iota(jnp.int32, (depth, depth), 1))
    weights = [-2.0 * w / FILTER_HALF for w in STENCIL_WEIGHTS]
    matrix = jnp.where(away == 0, 3.0 * weights[0] - FILTER_CENTER / FILTER_HALF, 0.0)
    for k in range(1, WIDTH + 1):
        matrix = jnp.where(away == k, weights[k], matrix)
    high = matrix.astype(jnp.bfloat16)
    band_ref[:depth, :] = high
    band_ref[depth:, :] = high
    rest_ref[...] = (matrix - high.astype(jnp.float32)).astype(jnp.bfloat16)


def inner_kernel(has_previous, field_ref, potential_ref, band_ref, rest_ref, *refs):
    previous_ref = refs[0] if has_previous else None
    total_ref = refs[-1]
    factor = 2.0 if has_previous else 1.0
    scale = factor / FILTER_HALF
    size_x, size_y, own, depth = field_ref.shape

    cells = field_ref[...].reshape(size_x * size_y * own, depth)
    high = cells.astype(jnp.bfloat16)
    low = (cells - high.astype(jnp.float32)).astype(jnp.bfloat16)
    along_z = jnp.dot(
        jnp.concatenate([high, low], axis=1), band_ref[...], preferred_element_type=jnp.float32
    ) + jnp.dot(high, rest_ref[...], preferred_element_type=jnp.float32)
    total_ref[...] = (factor * along_z).reshape(field_ref.shape)
    weights = [-2.0 * scale * w for w in STENCIL_WEIGHTS]

    def inside(total, line, at):
        for k in range(1, WIDTH + 1):
            near = [line[i] for i in (at - k, at + k) if 0 <= i < len(line)]
            if near:
                total = total + weights[k] * sum(near[1:], near[0])
        return total

    @pl.loop(0, size_y, unroll=4)
    def _(y):
        line = [field_ref[x, y] for x in range(size_x)]
        for x in range(size_x):
            total = total_ref[x, y]
            total = total + (scale * potential_ref[pl.ds(x * size_y + y, 1), :]) * line[x]
            if has_previous:
                total = total - previous_ref[x, y]
            total_ref[x, y] = inside(total, line, x)

    @pl.loop(0, size_x, unroll=4)
    def _(x):
        line = [field_ref[x, y] for y in range(size_y)]
        for y in range(size_y):
            total_ref[x, y] = inside(total_ref[x, y], line, y)


def add_side(right, halo, source, weights, store):
    size_x, size_y = source.shape[:2]

    @pl.loop(0, size_y, unroll=4)
    def _(y):
        line = [halo[k, y] for k in range(WIDTH)]
        for i in range(WIDTH):
            x = size_x - WIDTH + i if right else i
            total = source[x, y]
            for k in range(1, WIDTH + 1):
                if right and x + k >= size_x:
                    total = total + weights[k] * line[x + k - size_x]
                if not right and x - k < 0:
                    total = total + weights[k] * line[WIDTH + x - k]
            store(x, y, total)


def outer_first_kernel(factor, parity_ref, inner_ref, y_odd, x_even, y_even, total_ref, halo_x, halo_y):
    size_x, size_y, own, depth = inner_ref.shape
    weights = [-2.0 * factor / FILTER_HALF * w for w in STENCIL_WEIGHTS]
    odd = parity_ref[1]
    unpack(y_odd, halo_y, 1, odd * WIDTH, WIDTH - 1 + odd)
    unpack(y_even, halo_y, 1, (1 - odd) * WIDTH, WIDTH - odd)
    odd_x = parity_ref[0]
    unpack(x_even, halo_x, 0, 0, odd_x * (WIDTH - 1))

    @pl.loop(0, size_x, unroll=4)
    def _(x):
        line = [halo_y[x, k] for k in range(2 * WIDTH)]
        for y in range(size_y):
            total = inner_ref[x, y]
            for k in range(1, WIDTH + 1):
                if y - k < 0:
                    total = total + weights[k] * line[WIDTH + y - k]
                if y + k >= size_y:
                    total = total + weights[k] * line[WIDTH + y + k - size_y]
            total_ref[x, y] = total

    def store(x, y, total):
        total_ref[x, y] = total

    @pl.when(odd_x == 0)
    def _():
        add_side(True, halo_x, total_ref, weights, store)

    @pl.when(odd_x == 1)
    def _():
        add_side(False, halo_x, total_ref, weights, store)


def outer_last_kernel(factor, last, parity_ref, total_ref, x_odd, *refs):
    outs, halo_x = refs[:-1], refs[-1]
    size_x, size_y, own, depth = total_ref.shape
    weights = [-2.0 * factor / FILTER_HALF * w for w in STENCIL_WEIGHTS]
    odd_x = parity_ref[0]
    unpack(x_odd, halo_x, 0, 0, (1 - odd_x) * (WIDTH - 1))

    def store(x, y, total):
        if last:
            place = pl.multiple_of((x * size_y + y) * depth, depth)
            outs[0][:, pl.ds(place, depth)] = total
        else:
            outs[0][x, y] = total

    def keep(first):
        @pl.loop(0, size_y, unroll=4)
        def _(y):
            for x in range(first, first + size_x - WIDTH):
                store(x, y, total_ref[x, y])

    @pl.when(odd_x == 1)
    def _():
        add_side(True, halo_x, total_ref, weights, store)
        keep(0)

    @pl.when(odd_x == 0)
    def _():
        add_side(False, halo_x, total_ref, weights, store)
        keep(WIDTH)

    if not last:
        pack_messages(parity_ref, *outs)


def message_shapes(size_x, size_y, own, depth):
    short = max(WIDTH * size_x, SENT * size_y) * own
    long = SENT * size_x * own
    sizes = (long, max(long, short), (long + short) // 2 // 16 * 16, WIDTH * size_x * own)
    return [jax.ShapeDtypeStruct((rows, depth), jnp.bfloat16) for rows in sizes]


def params():
    return pltpu.CompilerParams(vmem_limit_bytes=VMEM_BYTES)


def in_vmem(count):
    return [pl.BlockSpec(memory_space=pltpu.VMEM)] * count


def start(parity, orbital_block):
    own, size_x, size_y, depth = orbital_block.shape
    field = jax.ShapeDtypeStruct((size_x, size_y, own, depth), jnp.float32)
    return pl.pallas_call(
        start_kernel,
        out_shape=[field] + message_shapes(size_x, size_y, own, depth),
        in_specs=[pl.BlockSpec(memory_space=pltpu.SMEM)] + in_vmem(1),
        out_specs=in_vmem(5),
        compiler_params=params(),
    )(parity, orbital_block.reshape(own * size_x * size_y, depth))


def fixed_arrays(potential):
    depth = potential.shape[1]
    return pl.pallas_call(
        fixed_kernel,
        out_shape=[
            jax.ShapeDtypeStruct(potential.shape, jnp.float32),
            jax.ShapeDtypeStruct((2 * depth, depth), jnp.bfloat16),
            jax.ShapeDtypeStruct((depth, depth), jnp.bfloat16),
        ],
        in_specs=in_vmem(1),
        out_specs=in_vmem(3),
        compiler_params=params(),
        cost_estimate=pl.CostEstimate(
            flops=30 * depth * depth, bytes_accessed=16 * depth * depth, transcendentals=0
        ),
    )(potential)


def filter_step(parity, field, fixed, messages, previous, last):
    size_x, size_y, own, depth = field.shape
    field_shape = jax.ShapeDtypeStruct(field.shape, jnp.float32)
    before = [] if previous is None else [previous]
    inner = pl.pallas_call(
        functools.partial(inner_kernel, previous is not None),
        out_shape=field_shape,
        in_specs=in_vmem(4 + len(before)),
        out_specs=in_vmem(1)[0],
        compiler_params=params(),
        cost_estimate=pl.CostEstimate(
            flops=6 * field.size * depth, bytes_accessed=12 * field.size, transcendentals=0
        ),
    )(field, *fixed, *before)
    y_odd, x_even, x_odd, y_even = messages
    factor = 1.0 if previous is None else 2.0
    scratch_x = pltpu.VMEM((WIDTH, size_y, own, depth), jnp.float32)
    scratch_y = pltpu.VMEM((size_x, 2 * WIDTH, own, depth), jnp.float32)
    smem = pl.BlockSpec(memory_space=pltpu.SMEM)
    total = pl.pallas_call(
        functools.partial(outer_first_kernel, factor),
        out_shape=field_shape,
        in_specs=[smem] + in_vmem(4),
        out_specs=in_vmem(1)[0],
        scratch_shapes=[scratch_x, scratch_y],
        compiler_params=params(),
        cost_estimate=pl.CostEstimate(
            flops=field.size, bytes_accessed=field.size, transcendentals=0
        ),
    )(parity, inner, y_odd, x_even, y_even)
    if last:
        out_shape = [jax.ShapeDtypeStruct((own, size_x * size_y * depth), jnp.float32)]
    else:
        out_shape = [field_shape] + message_shapes(size_x, size_y, own, depth)
    return pl.pallas_call(
        functools.partial(outer_last_kernel, factor, last),
        out_shape=out_shape,
        in_specs=[smem] + in_vmem(2),
        out_specs=in_vmem(len(out_shape)),
        scratch_shapes=[scratch_x],
        compiler_params=params(),
    )(parity, total, x_odd)


def swap(y_odd, x_even, x_odd, y_even):
    def swapped(values, axis, first):
        count = lax.axis_size(axis)
        step = lambda i: 1 if (i - first) % 2 == 0 else -1
        return lax.ppermute(values, axis, [(i, (i + step(i)) % count) for i in range(count)])

    return (
        swapped(y_odd, "dy", 1),
        swapped(x_even, "dx", 0),
        swapped(x_odd, "dx", 1),
        swapped(y_even, "dy", 0),
    )


def sum_over_grid(values, sent_type):
    for axis in ("dx", "dy"):
        count = lax.axis_size(axis)
        sent = jnp.broadcast_to(values.astype(sent_type)[None], (count,) + values.shape)
        values = jnp.sum(lax.all_to_all(sent, axis, 0, 0).astype(jnp.float32), axis=0)
    return values


def other_band(values):
    return lax.ppermute(values, "band", [(0, 1), (1, 0)])


def rows_dot(first, second, **kwargs):
    return lax.dot_general(
        first, second, (((1,), (1,)), ((), ())), preferred_element_type=jnp.float32, **kwargs
    )


def shards(orbital_block, potential, resident):
    own_count, size_x, size_y, depth = orbital_block.shape
    cell_count = size_x * size_y * depth
    flat_potential = potential.reshape(size_x * size_y, depth)
    parity = jnp.stack([lax.axis_index("dx") % 2, lax.axis_index("dy") % 2]).astype(jnp.int32)

    field, *messages = start(parity, orbital_block)
    fixed = fixed_arrays(flat_potential)
    previous = None
    for degree_step in range(DEGREE):
        last = degree_step == DEGREE - 1
        following, *messages = filter_step(
            parity, field, fixed, swap(*messages), previous, last
        )
        previous, field = field, following
    filtered = field

    rounded = filtered.astype(jnp.bfloat16)
    rounded_other = other_band(rounded)
    own_resident = resident.reshape(-1, cell_count)
    local_own = rows_dot(rounded, own_resident)
    local_other = rows_dot(rounded_other, own_resident)
    local = jnp.concatenate([local_own, local_other], axis=0) * SENT_SCALE
    correlations = (sum_over_grid(local, jnp.float16) / SENT_SCALE).astype(jnp.bfloat16)
    correction = jnp.dot(correlations, own_resident, preferred_element_type=jnp.float32)
    mine, theirs = correction[:own_count], correction[own_count:]
    got = other_band(theirs.astype(jnp.bfloat16)).astype(jnp.float32)
    got_other = other_band(mine.astype(jnp.bfloat16)).astype(jnp.float32)
    projected = filtered - mine - got
    projected_other = rounded_other.astype(jnp.float32) - theirs - got_other
    exact = functools.partial(rows_dot, precision=lax.Precision.HIGH)
    partial_gram = exact(projected, jnp.concatenate([projected, projected_other], axis=0))
    turned = jnp.roll(partial_gram, own_count, axis=1)
    partial_gram = jnp.where(lax.axis_index("band") == 0, partial_gram, turned)
    lanes = 128
    partial_gram = jnp.pad(partial_gram, ((0, 0), (0, lanes - 2 * own_count)))
    total_cells = cell_count * lax.axis_size("dx") * lax.axis_size("dy")
    gram_matrix = sum_over_grid(partial_gram, jnp.float32)[:, : 2 * own_count] / total_cells
    return (projected.reshape(orbital_block.shape), gram_matrix)


def solution(mesh):
    placed = (P("band", "dx", "dy", None), P("dx", "dy", None), P("band", "dx", "dy", None))
    return jax.shard_map(
        shards,
        mesh=mesh,
        in_specs=placed,
        out_specs=(P("band", "dx", "dy", None), P("band", None)),
        check_vma=False,
    )
```

```python
import functools

import jax
import jax.numpy as jnp
from jax import lax
from jax.experimental import pallas as pl
from jax.experimental.pallas import tpu as pltpu
from jax.sharding import PartitionSpec as P

DEGREE = 4


STENCIL_WEIGHTS = (
    -5369.0 / 1800.0,
    12.0 / 7.0,
    -15.0 / 56.0,
    10.0 / 189.0,
    -1.0 / 112.0,
    2.0 / 1925.0,
    -1.0 / 16632.0,
)
FILTER_CENTER = 23.0
FILTER_HALF = 21.0
WIDTH = 6
SENT = WIDTH + 1
SENT_SCALE = 1.0 / 64.0
VMEM_BYTES = 8 * 1024 * 1024


def pack_layer(out_ref, at, layer):
    rows = layer.shape[0] * layer.shape[1]
    out_ref[at * rows : (at + 1) * rows, :] = layer.reshape(rows, layer.shape[2]).astype(
        jnp.bfloat16
    )


def pack_messages(parity_ref, field_ref, y_odd, x_even, x_odd, y_even):
    def layer(dim, at):
        return field_ref[at] if dim == 0 else field_ref[:, at]

    for dim, even, odd in ((0, x_even, x_odd), (1, y_even, y_odd)):
        size = field_ref.shape[dim]
        for out_ref, tail in ((even, 1 - parity_ref[dim]), (odd, parity_ref[dim])):
            for at in range(WIDTH):
                pack_layer(out_ref, at, layer(dim, tail * (size - WIDTH) + at))
            nearest = layer(dim, tail * (size - 1))
            used = SENT * nearest.shape[0] * nearest.shape[1]
            if used > out_ref.shape[0]:
                continue
            pack_layer(out_ref, WIDTH, nearest - nearest.astype(jnp.bfloat16).astype(jnp.float32))
            if used < out_ref.shape[0]:
                rows = out_ref.shape[0] - used
                out_ref[used:, :] = jnp.zeros((rows, out_ref.shape[1]), jnp.bfloat16)


def unpack_messages(parity_ref, halo_x, halo_y, y_odd, x_even, x_odd, y_even):
    for dim, halo, even, odd in ((0, halo_x, x_even, x_odd), (1, halo_y, y_even, y_odd)):
        shape = halo.shape[1:] if dim == 0 else halo.shape[:1] + halo.shape[2:]
        rows = shape[0] * shape[1]
        parity = parity_ref[dim]
        for got, after, near in ((even, 1 - parity, WIDTH - parity), (odd, parity, WIDTH - 1 + parity)):
            def read(at):
                return got[at * rows : (at + 1) * rows, :].astype(jnp.float32).reshape(shape)

            for at in range(WIDTH):
                place = after * WIDTH + at
                if dim == 0:
                    halo[place] = read(at)
                else:
                    halo[:, place] = read(at)
            if got.shape[0] < SENT * rows:
                continue
            if dim == 0:
                halo[near] += read(WIDTH)
            else:
                halo[:, near] += read(WIDTH)


def start_kernel(parity_ref, cells_ref, field_ref, *messages):
    size_x, size_y, own = field_ref.shape[:3]
    for x in range(size_x):
        for y in range(size_y):
            rows = pl.ds(x * size_y + y, own, stride=size_x * size_y)
            field_ref[x, y] = cells_ref[rows, :]
    pack_messages(parity_ref, field_ref, *messages)


def fixed_kernel(potential_ref, kept_ref, band_ref, rest_ref):
    depth = rest_ref.shape[0]
    kept_ref[...] = potential_ref[...]
    row = lax.broadcasted_iota(jnp.int32, (depth, depth), 0)
    away = jnp.abs(row - lax.broadcasted_iota(jnp.int32, (depth, depth), 1))
    weights = [-2.0 * w / FILTER_HALF for w in STENCIL_WEIGHTS]
    matrix = jnp.where(away == 0, 3.0 * weights[0] - FILTER_CENTER / FILTER_HALF, 0.0)
    for k in range(1, WIDTH + 1):
        matrix = jnp.where(away == k, weights[k], matrix)
    high = matrix.astype(jnp.bfloat16)
    band_ref[:depth, :] = high
    band_ref[depth:, :] = high
    rest_ref[...] = (matrix - high.astype(jnp.float32)).astype(jnp.bfloat16)


def inner_kernel(has_previous, field_ref, potential_ref, band_ref, rest_ref, *refs):
    previous_ref = refs[0] if has_previous else None
    total_ref = refs[-1]
    factor = 2.0 if has_previous else 1.0
    scale = factor / FILTER_HALF
    size_x, size_y, own, depth = field_ref.shape

    cells = field_ref[...].reshape(size_x * size_y * own, depth)
    high = cells.astype(jnp.bfloat16)
    low = (cells - high.astype(jnp.float32)).astype(jnp.bfloat16)
    along_z = jnp.dot(
        jnp.concatenate([high, low], axis=1), band_ref[...], preferred_element_type=jnp.float32
    ) + jnp.dot(high, rest_ref[...], preferred_element_type=jnp.float32)
    total_ref[...] = (factor * along_z).reshape(field_ref.shape)
    weights = [-2.0 * scale * w for w in STENCIL_WEIGHTS]

    def inside(total, line, at):
        for k in range(1, WIDTH + 1):
            near = [line[i] for i in (at - k, at + k) if 0 <= i < len(line)]
            if near:
                total = total + weights[k] * sum(near[1:], near[0])
        return total

    @pl.loop(0, size_y, unroll=4)
    def _(y):
        line = [field_ref[x, y] for x in range(size_x)]
        for x in range(size_x):
            total = total_ref[x, y]
            total = total + (scale * potential_ref[pl.ds(x * size_y + y, 1), :]) * line[x]
            if has_previous:
                total = total - previous_ref[x, y]
            total_ref[x, y] = inside(total, line, x)

    @pl.loop(0, size_x, unroll=4)
    def _(x):
        line = [field_ref[x, y] for y in range(size_y)]
        for y in range(size_y):
            total_ref[x, y] = inside(total_ref[x, y], line, y)


def outer_kernel(factor, last, parity_ref, inner_ref, *refs):
    messages, outs, (halo_x, halo_y, total_ref) = refs[:4], refs[4:-3], refs[-3:]
    size_x, size_y, own, depth = inner_ref.shape
    unpack_messages(parity_ref, halo_x, halo_y, *messages)
    weights = [-2.0 * factor / FILTER_HALF * w for w in STENCIL_WEIGHTS]

    def outside(total, line, at, size):
        for k in range(1, WIDTH + 1):
            if at - k < 0:
                total = total + weights[k] * line[WIDTH + at - k]
            if at + k >= size:
                total = total + weights[k] * line[WIDTH + at + k - size]
        return total

    @pl.loop(0, size_y, unroll=4)
    def _(y):
        line = [halo_x[k, y] for k in range(2 * WIDTH)]
        for x in range(size_x):
            total_ref[x, y] = outside(inner_ref[x, y], line, x, size_x)

    @pl.loop(0, size_x, unroll=4)
    def _(x):
        line = [halo_y[x, k] for k in range(2 * WIDTH)]
        for y in range(size_y):
            total = outside(total_ref[x, y], line, y, size_y)
            if last:
                place = pl.multiple_of((x * size_y + y) * depth, depth)
                outs[0][:, pl.ds(place, depth)] = total
            else:
                outs[0][x, y] = total

    if not last:
        pack_messages(parity_ref, *outs)


def message_shapes(size_x, size_y, own, depth):
    short = max(WIDTH * size_x, SENT * size_y) * own
    sizes = (SENT * size_x * own, short, short, WIDTH * size_x * own)
    return [jax.ShapeDtypeStruct((rows, depth), jnp.bfloat16) for rows in sizes]


def params():
    return pltpu.CompilerParams(vmem_limit_bytes=VMEM_BYTES)


def in_vmem(count):
    return [pl.BlockSpec(memory_space=pltpu.VMEM)] * count


def start(parity, orbital_block):
    own, size_x, size_y, depth = orbital_block.shape
    field = jax.ShapeDtypeStruct((size_x, size_y, own, depth), jnp.float32)
    return pl.pallas_call(
        start_kernel,
        out_shape=[field] + message_shapes(size_x, size_y, own, depth),
        in_specs=[pl.BlockSpec(memory_space=pltpu.SMEM)] + in_vmem(1),
        out_specs=in_vmem(5),
        compiler_params=params(),
    )(parity, orbital_block.reshape(own * size_x * size_y, depth))


def fixed_arrays(potential):
    depth = potential.shape[1]
    return pl.pallas_call(
        fixed_kernel,
        out_shape=[
            jax.ShapeDtypeStruct(potential.shape, jnp.float32),
            jax.ShapeDtypeStruct((2 * depth, depth), jnp.bfloat16),
            jax.ShapeDtypeStruct((depth, depth), jnp.bfloat16),
        ],
        in_specs=in_vmem(1),
        out_specs=in_vmem(3),
        compiler_params=params(),
        cost_estimate=pl.CostEstimate(
            flops=30 * depth * depth, bytes_accessed=16 * depth * depth, transcendentals=0
        ),
    )(potential)


def filter_step(parity, field, fixed, messages, previous, last):
    size_x, size_y, own, depth = field.shape
    field_shape = jax.ShapeDtypeStruct(field.shape, jnp.float32)
    before = [] if previous is None else [previous]
    inner = pl.pallas_call(
        functools.partial(inner_kernel, previous is not None),
        out_shape=field_shape,
        in_specs=in_vmem(4 + len(before)),
        out_specs=in_vmem(1)[0],
        compiler_params=params(),
        cost_estimate=pl.CostEstimate(
            flops=6 * field.size * depth, bytes_accessed=12 * field.size, transcendentals=0
        ),
    )(field, *fixed, *before)
    if last:
        out_shape = [jax.ShapeDtypeStruct((own, size_x * size_y * depth), jnp.float32)]
    else:
        out_shape = [field_shape] + message_shapes(size_x, size_y, own, depth)
    return pl.pallas_call(
        functools.partial(outer_kernel, 1.0 if previous is None else 2.0, last),
        out_shape=out_shape,
        in_specs=[pl.BlockSpec(memory_space=pltpu.SMEM)] + in_vmem(5),
        out_specs=in_vmem(len(out_shape)),
        scratch_shapes=[
            pltpu.VMEM((2 * WIDTH, size_y, own, depth), jnp.float32),
            pltpu.VMEM((size_x, 2 * WIDTH, own, depth), jnp.float32),
            pltpu.VMEM(field.shape, jnp.float32),
        ],
        compiler_params=params(),
    )(parity, inner, *messages)


def swap(y_odd, x_even, x_odd, y_even):
    def swapped(values, axis, first):
        count = lax.axis_size(axis)
        step = lambda i: 1 if (i - first) % 2 == 0 else -1
        return lax.ppermute(values, axis, [(i, (i + step(i)) % count) for i in range(count)])

    return (
        swapped(y_odd, "dy", 1),
        swapped(x_even, "dx", 0),
        swapped(x_odd, "dx", 1),
        swapped(y_even, "dy", 0),
    )


def sum_over_grid(values, sent_type):
    for axis in ("dx", "dy"):
        count = lax.axis_size(axis)
        sent = jnp.broadcast_to(values.astype(sent_type)[None], (count,) + values.shape)
        values = jnp.sum(lax.all_to_all(sent, axis, 0, 0).astype(jnp.float32), axis=0)
    return values


def other_band(values):
    return lax.ppermute(values, "band", [(0, 1), (1, 0)])


def rows_dot(first, second, **kwargs):
    return lax.dot_general(
        first, second, (((1,), (1,)), ((), ())), preferred_element_type=jnp.float32, **kwargs
    )


def shards(orbital_block, potential, resident):
    own_count, size_x, size_y, depth = orbital_block.shape
    cell_count = size_x * size_y * depth
    flat_potential = potential.reshape(size_x * size_y, depth)
    parity = jnp.stack([lax.axis_index("dx") % 2, lax.axis_index("dy") % 2]).astype(jnp.int32)

    field, *messages = start(parity, orbital_block)
    fixed = fixed_arrays(flat_potential)
    previous = None
    for degree_step in range(DEGREE):
        last = degree_step == DEGREE - 1
        following, *messages = filter_step(
            parity, field, fixed, swap(*messages), previous, last
        )
        previous, field = field, following
    filtered = field

    rounded = filtered.astype(jnp.bfloat16)
    rounded_other = other_band(rounded)
    own_resident = resident.reshape(-1, cell_count)
    local_own = rows_dot(rounded, own_resident)
    local_other = rows_dot(rounded_other, own_resident)
    local = jnp.concatenate([local_own, local_other], axis=0) * SENT_SCALE
    correlations = (sum_over_grid(local, jnp.float16) / SENT_SCALE).astype(jnp.bfloat16)
    correction = jnp.dot(correlations, own_resident, preferred_element_type=jnp.float32)
    mine, theirs = correction[:own_count], correction[own_count:]
    got = other_band(theirs.astype(jnp.bfloat16)).astype(jnp.float32)
    got_other = other_band(mine.astype(jnp.bfloat16)).astype(jnp.float32)
    projected = filtered - mine - got
    projected_other = rounded_other.astype(jnp.float32) - theirs - got_other
    exact = functools.partial(rows_dot, precision=lax.Precision.HIGH)
    partial_gram = exact(projected, jnp.concatenate([projected, projected_other], axis=0))
    turned = jnp.roll(partial_gram, own_count, axis=1)
    partial_gram = jnp.where(lax.axis_index("band") == 0, partial_gram, turned)
    lanes = 128
    partial_gram = jnp.pad(partial_gram, ((0, 0), (0, lanes - 2 * own_count)))
    total_cells = cell_count * lax.axis_size("dx") * lax.axis_size("dy")
    gram_matrix = sum_over_grid(partial_gram, jnp.float32)[:, : 2 * own_count] / total_cells
    return (projected.reshape(orbital_block.shape), gram_matrix)


def solution(mesh):
    placed = (P("band", "dx", "dy", None), P("dx", "dy", None), P("band", "dx", "dy", None))
    return jax.shard_map(
        shards,
        mesh=mesh,
        in_specs=placed,
        out_specs=(P("band", "dx", "dy", None), P("band", None)),
        check_vma=False,
    )
```
